256 devices in a mesh: img: 4 (over x_lo, core), prm: 64 (over x_hi, y, z).
Axes of the slice: x: 4 (x_hi: 2, x_lo: 2; x = x_hi * 2 + x_lo), y: 4, z: 8, core: 2. Of those that a mesh axis runs over, the one named last changes fastest.
Arguments:
- teacher_maps: bfloat16 [16, 1024, 1152], P('img', 'prm'), may hold values from -6 to 6
- pool_index: int32 [256, 4], replicated, may hold values from 0 to 1023, as said below
- pairing: int32 [16], P('img'), may hold values from 0 to 15, as said below
- teacher_prompts: bfloat16 [32768, 1152], P('prm')
- student_patches: bfloat16 [16, 256, 768], P('img'), may hold values from -9 to 9
- student_prompts: bfloat16 [32768, 768], P('prm')
Outputs:
- patch_kl: float32 [16, 256], P('img')
- patch_grad: bfloat16 [16, 256, 768], P('img')
The draws below stay inside these ranges and needn't reach their ends.
Inputs may be any that keep to these rules, and one draw needn't show every extreme that they name: pool_index[q, j] = r * 32 + c with grid row r within 2 * (q // 16) - 1 to 2 * (q // 16) + 2 and grid column c within 2 * (q % 16) - 1 to 2 * (q % 16) + 2, both inside the grid. `pairing`: a permutation of the 16 images.
All inputs are finite; a program needn't handle non-finite values.
Results may differ from the reference program's by a relative error of at most 0.001.
The reference program's roundings to bfloat16 on the way (of `pooled` and `difference`) count: a program that leaves them out, or rounds other values in their place, can miss the bound.
Values may be sent and summed in bfloat16 or wider, within the bound.
No kernel may reach another device: no remote copies, remote signals or barrier semaphores. Data moves between devices by JAX's collectives and lax.ppermute only.
A program may use at most 64 MiB of HBM per device.

```python
import jax
import jax.numpy as jnp
from jax import lax

D_T = 1152
D_S = 768
SIDE = 32
GRID = 1024
POOLED = 256
IMAGES = 16
PROMPTS = 32768


def anchor_rows(key, width, salt):
    return jnp.clip(jax.random.normal(jax.random.fold_in(key, salt), (4, width), jnp.float32), -3.0, 3.0)


def draw_teacher_maps(key, part):
    anchor = anchor_rows(key, D_T, 101)
    key = jax.random.fold_in(key, 1)
    values = jnp.clip(jax.random.normal(key, (IMAGES, GRID, D_T), jnp.float32), -4.5, 4.5)
    strengths = [1.0, 1.3, 1.6, 2.0]
    for number in range(min(4, IMAGES)):
        values = values.at[number, 0:3 * SIDE].set(jnp.broadcast_to(anchor[number] * strengths[number], (3 * SIDE, D_T)))
    return values.astype(jnp.bfloat16)


def draw_teacher_prompts(key, part):
    anchor = anchor_rows(key, D_T, 101)
    key = jax.random.fold_in(key, 2)
    factor = 6.0 * D_T ** (-0.5)
    values = jnp.clip(jax.random.normal(key, (PROMPTS, D_T), jnp.float32), -4.5, 4.5) * factor
    big = 120.0 / D_T
    for number in range(4):
        values = values.at[PROMPTS - 8 + 2 * number].set(anchor[number] * big)
        values = values.at[PROMPTS - 7 + 2 * number].set(anchor[number] * big * 0.99)
    return values.astype(jnp.bfloat16)


def draw_student_patches(key, part):
    anchor = anchor_rows(key, D_S, 202)
    key = jax.random.fold_in(key, 3)
    values = jnp.clip(jax.random.normal(key, (IMAGES, POOLED, D_S), jnp.float32), -4.5, 4.5)
    strengths = [1.3, 1.8, 2.4, 3.0]
    for number in range(4):
        values = values.at[0, number].set(anchor[number] * strengths[number])
    return values.astype(jnp.bfloat16)


def draw_student_prompts(key, part):
    anchor = anchor_rows(key, D_S, 202)
    key = jax.random.fold_in(key, 4)
    factor = 3.0 * D_S ** (-0.5)
    values = jnp.clip(jax.random.normal(key, (PROMPTS, D_S), jnp.float32), -4.5, 4.5) * factor
    big = 120.0 / D_S
    for number in range(4):
        values = values.at[PROMPTS - 8 + 2 * number].set(anchor[number] * big)
        values = values.at[PROMPTS - 7 + 2 * number].set(anchor[number] * big * 0.992)
    return values.astype(jnp.bfloat16)


def draw_pool_index(key, part):
    key = jax.random.fold_in(key, 5)
    half_side = SIDE // 2
    cell_number = jnp.arange(POOLED, dtype=jnp.int32)
    row_base = 2 * (cell_number // half_side)
    col_base = 2 * (cell_number % half_side)
    offsets = jax.random.randint(key, (POOLED, 4, 2), -1, 3, dtype=jnp.int32)
    row_pick = jnp.clip(row_base[:, None] + offsets[:, :, 0], 0, SIDE - 1)
    col_pick = jnp.clip(col_base[:, None] + offsets[:, :, 1], 0, SIDE - 1)
    return (row_pick * SIDE + col_pick).astype(jnp.int32)


def draw_pairing(key, part):
    key = jax.random.fold_in(key, 6)
    return jax.random.permutation(key, IMAGES).astype(jnp.int32)


def setup_inputs(seed: int = 0) -> dict:
    arg_keys = jax.random.split(jax.random.key(seed), 7)
    return {
        "teacher_maps": draw_teacher_maps(jax.random.fold_in(arg_keys[6], 71), 0),
        "pool_index": draw_pool_index(jax.random.fold_in(arg_keys[6], 71), 0),
        "pairing": draw_pairing(jax.random.fold_in(arg_keys[6], 71), 0),
        "teacher_prompts": draw_teacher_prompts(jax.random.fold_in(arg_keys[6], 71), 0),
        "student_patches": draw_student_patches(jax.random.fold_in(arg_keys[6], 71), 0),
        "student_prompts": draw_student_prompts(jax.random.fold_in(arg_keys[6], 71), 0),
    }


def scores(rows_in, prompts):
    return lax.dot_general(rows_in, prompts, (((1,), (1,)), ((), ())), preferred_element_type=jnp.float32)


def reference(teacher_maps, pool_index, pairing, teacher_prompts, student_patches, student_prompts):
    def per_image(pieces):
        teacher_index, student_rows = pieces
        whole_map = lax.dynamic_index_in_dim(teacher_maps, teacher_index, 0, keepdims=False)
        picked = jnp.take(whole_map, pool_index.reshape(-1), axis=0).astype(jnp.float32)
        pooled = (picked.reshape(POOLED, 4, D_T).sum(1) * 0.25).astype(jnp.bfloat16)
        teacher_logits = scores(pooled, teacher_prompts)
        student_logits = scores(student_rows, student_prompts)
        max_teacher = jnp.max(teacher_logits, axis=1)
        max_student = jnp.max(student_logits, axis=1)
        exp_teacher = jnp.exp(teacher_logits - max_teacher[:, None])
        exp_student = jnp.exp(student_logits - max_student[:, None])
        sum_teacher = jnp.sum(exp_teacher, axis=1)
        sum_student = jnp.sum(exp_student, axis=1)
        numerator = jnp.sum(exp_teacher * (teacher_logits - student_logits), axis=1)
        kl_rows = numerator / sum_teacher - max_teacher - jnp.log(sum_teacher) + max_student + jnp.log(sum_student)
        difference = (exp_student / sum_student[:, None] - exp_teacher / sum_teacher[:, None]).astype(jnp.bfloat16)
        grad_rows = jnp.dot(difference, student_prompts, preferred_element_type=jnp.float32).astype(jnp.bfloat16)
        return kl_rows, grad_rows

    patch_kl, patch_grad = lax.map(per_image, (pairing.astype(jnp.int32), student_patches))
    return patch_kl, patch_grad
```

```python
import jax
import jax.numpy as jnp
from jax import lax
from jax.sharding import Mesh, PartitionSpec as P

IMG = ("xlo", "core")
PRM = ("xhi", "y", "z")
F32 = jnp.float32
BF16 = jnp.bfloat16


def scores(rows_in, prompts):
    return lax.dot_general(
        rows_in, prompts, (((1,), (1,)), ((), ())), preferred_element_type=F32
    )


def swap(x, axis, size):
    return lax.all_to_all(x, axis, split_axis=0, concat_axis=0, tiled=True)


def spread(x, axis, size):
    return swap(jnp.broadcast_to(x[None], (size,) + x.shape), axis, size)


def merge(stats):
    max_t = jnp.max(stats[:, 0], axis=0)
    max_s = jnp.max(stats[:, 3], axis=0)
    weight_t = jnp.exp(stats[:, 0] - max_t)
    weight_s = jnp.exp(stats[:, 3] - max_s)
    return jnp.stack(
        [
            max_t,
            jnp.sum(stats[:, 1] * weight_t, axis=0),
            jnp.sum(stats[:, 2] * weight_t, axis=0),
            max_s,
            jnp.sum(stats[:, 4] * weight_s, axis=0),
        ]
    )


def body(teacher_maps, pool_index, pairing, teacher_prompts, student_patches, student_prompts):
    n_xhi, n_y, n_z = (lax.axis_size(a) for a in PRM)
    n_w = n_xhi * n_y
    xhi, z = lax.axis_index("xhi"), lax.axis_index("z")
    w = xhi * n_y + lax.axis_index("y")
    half = z % 2

    other = [(0, 1), (1, 0)]
    student_other = lax.ppermute(student_prompts, "xhi", other)
    teacher_other = lax.ppermute(teacher_prompts, "xhi", other)

    patches = student_patches.reshape(4, n_xhi, n_y, 2, 16, -1)
    patches = lax.dynamic_index_in_dim(patches, xhi, 1, keepdims=False)
    student_rows = patches.transpose(1, 0, 2, 3, 4).reshape(n_y * 128, -1)

    every_map = lax.all_gather(teacher_maps, IMG, axis=0, tiled=True)
    owned = jnp.stack(
        [lax.dynamic_index_in_dim(every_map, pairing[j], 0, keepdims=False) for j in range(4)]
    )
    pairs = [((v + 1) * n_z + c, v * n_z + c) for v in range(n_w - 1) for c in (0, 1)]
    pairs += [(v * n_z + c, (v + 1) * n_z + c) for v in range(n_w - 1) for c in (6, 7)]
    halo = lax.ppermute(owned, PRM, pairs)
    to_upper = jnp.where(z >= 6, halo, owned)
    to_lower = jnp.where(z <= 1, halo, owned)
    cells = swap(jnp.stack([to_upper, to_lower], axis=1).reshape((8,) + owned.shape[1:]), "z", n_z)
    cells = cells.reshape(128, -1)
    source = jnp.arange(8)
    grid_row = 4 * w + source // 2
    grid_row = jnp.where(
        half == 0,
        jnp.where(source >= 6, 4 * w - 1, grid_row),
        jnp.where(source <= 1, 4 * w + 4, grid_row),
    )
    cell_id = grid_row[:, None] * 32 + (source % 2)[:, None] * 16 + jnp.arange(16)[None]
    cell_id = cell_id.reshape(-1)
    index = lax.dynamic_slice_in_dim(pool_index, 16 * (2 * w + half), 16, 0)
    counts = jnp.sum((index[:, :, None] == cell_id[None, None, :]).astype(F32), axis=1)
    pooled = (jnp.dot(counts.astype(BF16), cells, preferred_element_type=F32) * 0.25).astype(BF16)

    pooled = spread(pooled, "z", n_z).reshape(128, -1)
    pooled = spread(pooled, "y", n_y).reshape(n_y * 128, -1)

    prompts_t = jnp.concatenate([teacher_prompts, teacher_other])
    prompts_s = jnp.concatenate([student_prompts, student_other])
    teacher_logits = scores(pooled, prompts_t)
    student_logits = scores(student_rows, prompts_s)
    max_t = jnp.max(teacher_logits, axis=1)
    max_s = jnp.max(student_logits, axis=1)
    exp_t = jnp.exp(teacher_logits - max_t[:, None])
    exp_s = jnp.exp(student_logits - max_s[:, None])
    stats = jnp.stack(
        [
            max_t,
            jnp.sum(exp_t, axis=1),
            jnp.sum(exp_t * (teacher_logits - student_logits), axis=1),
            max_s,
            jnp.sum(exp_s, axis=1),
        ]
    )
    total = merge(spread(stats, ("y", "z"), n_y * n_z))
    all_max_t, sum_t, numerator, all_max_s, sum_s = (total[i] for i in range(5))
    kl_rows = numerator / sum_t - all_max_t - jnp.log(sum_t) + all_max_s + jnp.log(sum_s)
    scale_t = jnp.exp(max_t - all_max_t) / sum_t
    scale_s = jnp.exp(max_s - all_max_s) / sum_s
    difference = (exp_s * scale_s[:, None] - exp_t * scale_t[:, None]).astype(BF16)
    grad_term = jnp.dot(difference, prompts_s, preferred_element_type=F32)

    grad = jnp.sum(swap(grad_term.reshape(n_y, 128, -1), "y", n_y), axis=0)
    grad = jnp.sum(swap(grad.reshape(n_z, 16, -1), "z", n_z), axis=0).astype(BF16)
    grad = spread(grad, "z", n_z)
    grad = spread(grad, ("xhi", "y"), n_w)
    patch_grad = grad.reshape(n_w, 4, 2, 16, -1).transpose(1, 0, 2, 3, 4)

    kl_other = lax.ppermute(kl_rows, "xhi", other)
    kl = jnp.where(xhi == 0, jnp.stack([kl_rows, kl_other]), jnp.stack([kl_other, kl_rows]))
    patch_kl = kl.reshape(n_w, 4, 2, 16).transpose(1, 0, 2, 3).reshape(4, -1)
    return patch_kl, patch_grad.reshape(student_patches.shape)


def solution(mesh):
    split = Mesh(mesh.devices.reshape(2, 2, 2, 4, 8), IMG + PRM)
    placed = (
        P(IMG, PRM, None),
        P(),
        P(IMG),
        P(PRM, None),
        P(IMG, None, None),
        P(PRM, None),
    )
    return jax.shard_map(
        body,
        mesh=split,
        in_specs=placed,
        out_specs=(P(IMG, None), P(IMG, None, None)),
        check_vma=False,
    )
```

```python
import functools

import jax
import jax.numpy as jnp
from jax import lax
from jax.experimental import pallas as pl
from jax.experimental.pallas import tpu as pltpu
from jax.sharding import Mesh, PartitionSpec as P

IMG = ("xlo", "core")
PRM = ("xhi", "y", "zh", "zl")
Z = ("zh", "zl")
F32 = jnp.float32
BF16 = jnp.bfloat16
D_T = 1152
D_S = 768
PIECE = 256
ROWS = 256
CONTRACT_LAST = (((1,), (1,)), ((), ()))
CONTRACT_FIRST = (((0,), (0,)), ((), ()))


def swap(x, axis):
    return lax.all_to_all(x, axis, split_axis=0, concat_axis=0, tiled=True)


def spread(x, axis, size):
    return swap(jnp.broadcast_to(x[None], (size,) + x.shape), axis)


def score_kernel(pooled, student, own_t, own_s, got, swapped, exp_t, exp_s, piece, total):
    step = pl.program_id(0)

    def work(prompts_t, prompts_s):
        logits_t = lax.dot_general(prompts_t, pooled[...], CONTRACT_LAST, preferred_element_type=F32)
        logits_s = lax.dot_general(prompts_s, student[...], CONTRACT_LAST, preferred_element_type=F32)
        max_t = jnp.max(logits_t, axis=0, keepdims=True)
        max_s = jnp.max(logits_s, axis=0, keepdims=True)
        e_t = jnp.exp(logits_t - max_t)
        e_s = jnp.exp(logits_s - max_s)
        exp_t[...] = e_t
        exp_s[...] = e_s
        sum_t = jnp.sum(e_t, axis=0, keepdims=True)
        number = jnp.sum(e_t * (logits_t - logits_s), axis=0, keepdims=True)
        sum_s = jnp.sum(e_s, axis=0, keepdims=True)
        piece[0, 0:1] = max_t
        piece[0, 1:2] = max_s

        @pl.when(step == 0)
        def _():
            total[...] = jnp.zeros_like(total)
            for i, v in enumerate((max_t, sum_t, number, max_s, sum_s)):
                total[i : i + 1] = v

        @pl.when(step > 0)
        def _():
            top_t = jnp.maximum(total[0:1], max_t)
            top_s = jnp.maximum(total[3:4], max_s)
            old_t, new_t = jnp.exp(total[0:1] - top_t), jnp.exp(max_t - top_t)
            old_s, new_s = jnp.exp(total[3:4] - top_s), jnp.exp(max_s - top_s)
            total[1:2] = total[1:2] * old_t + sum_t * new_t
            total[2:3] = total[2:3] * old_t + number * new_t
            total[4:5] = total[4:5] * old_s + sum_s * new_s
            total[0:1] = top_t
            total[3:4] = top_s

    @pl.when(step < 2)
    def _():
        work(own_t[...], own_s[...])

    @pl.when((step >= 2) & (step < 5))
    def _():
        work(got[:, :D_T], got[:, D_T:])

    @pl.when(step >= 5)
    def _():
        work(swapped[:, :D_T], swapped[:, D_T:])


def score(pooled, student, own_t, own_s, got, swapped):
    whole = lambda i: (0, 0)
    own = lambda i: (jnp.minimum(i, 1), 0)
    first = lambda i: (jnp.clip(i - 2, 0, 2), 0)
    second = lambda i: (jnp.clip(i - 5, 0, 2), 0)
    return pl.pallas_call(
        score_kernel,
        grid=(8,),
        in_specs=[
            pl.BlockSpec((ROWS, D_T), whole),
            pl.BlockSpec((ROWS, D_S), whole),
            pl.BlockSpec((PIECE, D_T), own),
            pl.BlockSpec((PIECE, D_S), own),
            pl.BlockSpec((PIECE, D_T + D_S), first),
            pl.BlockSpec((PIECE, D_T + D_S), second),
        ],
        out_specs=[
            pl.BlockSpec((PIECE, ROWS), lambda i: (i, 0)),
            pl.BlockSpec((PIECE, ROWS), lambda i: (i, 0)),
            pl.BlockSpec((1, 8, ROWS), lambda i: (i, 0, 0)),
            pl.BlockSpec((8, ROWS), whole),
        ],
        out_shape=[
            jax.ShapeDtypeStruct((8 * PIECE, ROWS), F32),
            jax.ShapeDtypeStruct((8 * PIECE, ROWS), F32),
            jax.ShapeDtypeStruct((8, 8, ROWS), F32),
            jax.ShapeDtypeStruct((8, ROWS), F32),
        ],
        cost_estimate=pl.CostEstimate(
            flops=2 * 8 * PIECE * ROWS * (D_T + D_S), bytes_accessed=13 << 20, transcendentals=0
        ),
        name="score",
    )(pooled, student, own_t, own_s, got, swapped)


def grad_kernel(exp_t, exp_s, piece, stats, own_s, got, swapped, grad, kl, scale):
    step = pl.program_id(0)

    @pl.when(step == 0)
    def _():
        every = stats[...]
        top_t = jnp.max(every[:, 0], axis=0, keepdims=True)
        top_s = jnp.max(every[:, 3], axis=0, keepdims=True)
        weight_t = jnp.exp(every[:, 0] - top_t)
        weight_s = jnp.exp(every[:, 3] - top_s)
        sum_t = jnp.sum(every[:, 1] * weight_t, axis=0, keepdims=True)
        number = jnp.sum(every[:, 2] * weight_t, axis=0, keepdims=True)
        sum_s = jnp.sum(every[:, 4] * weight_s, axis=0, keepdims=True)
        kl[...] = number / sum_t - top_t - jnp.log(sum_t) + top_s + jnp.log(sum_s)
        scale[0:1] = top_t
        scale[1:2] = sum_t
        scale[2:3] = top_s
        scale[3:4] = sum_s
        grad[...] = jnp.zeros_like(grad)

    scale_t = jnp.exp(piece[0, 0:1] - scale[0:1]) / scale[1:2]
    scale_s = jnp.exp(piece[0, 1:2] - scale[2:3]) / scale[3:4]
    difference = (exp_s[...] * scale_s - exp_t[...] * scale_t).astype(BF16)

    def work(prompts_s):
        grad[...] += lax.dot_general(difference, prompts_s, CONTRACT_FIRST, preferred_element_type=F32)

    @pl.when(step < 2)
    def _():
        work(own_s[...])

    @pl.when((step >= 2) & (step < 5))
    def _():
        work(got[:, D_T:])

    @pl.when(step >= 5)
    def _():
        work(swapped[:, D_T:])


def gradient(exp_t, exp_s, piece, stats, own_s, got, swapped):
    whole = lambda i: (0, 0)
    own = lambda i: (jnp.minimum(i, 1), 0)
    first = lambda i: (jnp.clip(i - 2, 0, 2), 0)
    second = lambda i: (jnp.clip(i - 5, 0, 2), 0)
    return pl.pallas_call(
        grad_kernel,
        grid=(8,),
        in_specs=[
            pl.BlockSpec((PIECE, ROWS), lambda i: (i, 0)),
            pl.BlockSpec((PIECE, ROWS), lambda i: (i, 0)),
            pl.BlockSpec((1, 8, ROWS), lambda i: (i, 0, 0)),
            pl.BlockSpec(stats.shape, lambda i: (0, 0, 0)),
            pl.BlockSpec((PIECE, D_S), own),
            pl.BlockSpec((PIECE, D_T + D_S), first),
            pl.BlockSpec((PIECE, D_T + D_S), second),
        ],
        out_specs=[pl.BlockSpec((ROWS, D_S), whole), pl.BlockSpec((1, ROWS), whole)],
        out_shape=[
            jax.ShapeDtypeStruct((ROWS, D_S), F32),
            jax.ShapeDtypeStruct((1, ROWS), F32),
        ],
        scratch_shapes=[pltpu.VMEM((8, ROWS), F32)],
        cost_estimate=pl.CostEstimate(
            flops=2 * 8 * PIECE * ROWS * D_S, bytes_accessed=10 << 20, transcendentals=0
        ),
        name="gradient",
    )(exp_t, exp_s, piece, stats, own_s, got, swapped)


def body(teacher_maps, pool_index, pairing, teacher_prompts, student_patches, student_prompts):
    n_w, n_z = 8, 8
    xhi, zh, zl = (lax.axis_index(a) for a in ("xhi", "zh", "zl"))
    w = xhi * 4 + lax.axis_index("y")
    z = zh * 2 + zl

    core = lax.axis_index("core")
    half = jnp.concatenate(
        [
            lax.dynamic_slice_in_dim(teacher_prompts, core * PIECE, PIECE, 0),
            lax.dynamic_slice_in_dim(student_prompts, core * PIECE, PIECE, 0),
        ],
        axis=1,
    )
    flip1, flip2, flip3 = ([(i, n - 1 - i) for i in range(n)] for n in (2, 4, 8))
    got = [
        lax.ppermute(half, ("xlo", "xhi"), flip2),
        lax.ppermute(half, ("zl",), flip1),
        lax.ppermute(half, ("xlo", "xhi", "zl"), flip3),
    ]

    patches = student_patches.reshape(4, 2, 4, 2, 16, D_S)
    patches = lax.dynamic_index_in_dim(patches, xhi, 1, keepdims=False)
    patches = lax.dynamic_index_in_dim(patches, zl, 2, keepdims=False)
    student_rows = patches.transpose(1, 0, 2, 3).reshape(ROWS, D_S)

    every_map = lax.all_gather(teacher_maps, IMG, axis=0, tiled=True)
    owned = jnp.stack(
        [lax.dynamic_index_in_dim(every_map, pairing[j], 0, keepdims=False) for j in range(4)]
    )
    pairs = [((v + 1) * n_z + c, v * n_z + c) for v in range(n_w - 1) for c in (0, 1)]
    pairs += [(v * n_z + c, (v + 1) * n_z + c) for v in range(n_w - 1) for c in (6, 7)]
    halo = lax.ppermute(owned, PRM, pairs)
    to_upper = jnp.where(z >= 6, halo, owned)
    to_lower = jnp.where(z <= 1, halo, owned)
    cells = swap(jnp.stack([to_upper, to_lower], axis=1).reshape((8,) + owned.shape[1:]), Z)
    cells = cells.reshape(128, D_T)
    source = jnp.arange(8)
    grid_row = 4 * w + source // 2
    grid_row = jnp.where(
        zl == 0,
        jnp.where(source >= 6, 4 * w - 1, grid_row),
        jnp.where(source <= 1, 4 * w + 4, grid_row),
    )
    cell_id = grid_row[:, None] * 32 + (source % 2)[:, None] * 16 + jnp.arange(16)[None]
    cell_id = cell_id.reshape(-1)
    index = lax.dynamic_slice_in_dim(pool_index, 16 * (2 * w + zl), 16, 0)
    counts = jnp.sum((index[:, :, None] == cell_id[None, None, :]).astype(F32), axis=1)
    cells, *got = lax.optimization_barrier((cells, *got))
    got = jnp.concatenate(got)
    swapped = lax.ppermute(got, "core", flip1)
    pooled = (jnp.dot(counts.astype(BF16), cells, preferred_element_type=F32) * 0.25).astype(BF16)

    pooled = spread(pooled, "zh", 4).reshape(64, D_T)
    pooled = spread(pooled, "y", 4).reshape(ROWS, D_T)

    exp_t, exp_s, piece, total = score(
        pooled, student_rows, teacher_prompts, student_prompts, got, swapped
    )
    stats = spread(total, ("y", "zh"), 16)
    grad_term, kl_rows = gradient(exp_t, exp_s, piece, stats, student_prompts, got, swapped)

    grad = jnp.sum(swap(grad_term.reshape(4, 64, D_S), "y"), axis=0)
    grad = jnp.sum(swap(grad.reshape(4, 16, D_S), "zh"), axis=0).astype(BF16)
    grad = spread(grad, Z, n_z)
    grad = spread(grad, ("xhi", "y"), n_w)
    patch_grad = grad.reshape(n_w, 4, 2, 16, D_S).transpose(1, 0, 2, 3, 4)

    kl = spread(kl_rows.reshape(4, 4, 16), ("xhi", "zl"), 4)
    patch_kl = kl.reshape(2, 2, 4, 4, 16).transpose(3, 0, 2, 1, 4).reshape(4, -1)
    return patch_kl, patch_grad.reshape(student_patches.shape)


def solution(mesh):
    split = Mesh(mesh.devices.reshape(2, 2, 2, 4, 4, 2), IMG + PRM)
    placed = (
        P(IMG, PRM, None),
        P(),
        P(IMG),
        P(PRM, None),
        P(IMG, None, None),
        P(PRM, None),
    )
    return jax.shard_map(
        body,
        mesh=split,
        in_specs=placed,
        out_specs=(P(IMG, None), P(IMG, None, None)),
        check_vma=False,
    )
```

```python
import functools

import jax
import jax.numpy as jnp
from jax import lax
from jax.experimental import pallas as pl
from jax.experimental.pallas import tpu as pltpu
from jax.sharding import Mesh, PartitionSpec as P

IMG = ("xlo", "core")
PRM = ("xhi", "y", "zh", "zl")
Z = ("zh", "zl")
F32 = jnp.float32
BF16 = jnp.bfloat16
D_T = 1152
D_S = 768
PIECE = 256
ROWS = 256
CONTRACT_LAST = (((1,), (1,)), ((), ()))
CONTRACT_FIRST = (((0,), (0,)), ((), ()))


def swap(x, axis):
    return lax.all_to_all(x, axis, split_axis=0, concat_axis=0, tiled=True)


def spread(x, axis, size):
    return swap(jnp.broadcast_to(x[None], (size,) + x.shape), axis)


def score_kernel(pooled, student, own_t, own_s, *refs):
    got, (exp_t, exp_s, prompts, total, teacher, sems) = refs[:6], refs[6:]
    copies = []

    def copy(source, target):
        copies.append(pltpu.make_async_copy(source, target, sems.at[len(copies)]))
        copies[-1].start()

    copy(own_t, teacher.at[0 : 2 * PIECE])
    copy(own_s, prompts.at[0 : 2 * PIECE])
    for i, piece in enumerate(got):
        at = (2 + i) * PIECE
        copy(piece.at[:, 0:D_T], teacher.at[at : at + PIECE])
        copy(piece.at[:, D_T : D_T + D_S], prompts.at[at : at + PIECE])

    spans = [(0, 2 * PIECE, copies[:2]), (2 * PIECE, 8 * PIECE, copies[2:])]
    logits = []
    for first, last, needed in spans:
        for c in needed:
            c.wait()
        logits.append(
            (
                lax.dot_general(
                    teacher[first:last], pooled[...], CONTRACT_LAST, preferred_element_type=F32
                ),
                lax.dot_general(
                    prompts[first:last], student[...], CONTRACT_LAST, preferred_element_type=F32
                ),
            )
        )
    max_t, max_s = (
        functools.reduce(jnp.maximum, [jnp.max(both[i], axis=0, keepdims=True) for both in logits])
        for i in range(2)
    )
    sum_t = number = sum_s = 0.0
    for (first, last, _), (logits_t, logits_s) in zip(spans, logits):
        e_t = jnp.exp(logits_t - max_t)
        e_s = jnp.exp(logits_s - max_s)
        exp_t[first:last] = e_t
        exp_s[first:last] = e_s
        sum_t += jnp.sum(e_t, axis=0, keepdims=True)
        number += jnp.sum(e_t * (logits_t - logits_s), axis=0, keepdims=True)
        sum_s += jnp.sum(e_s, axis=0, keepdims=True)
    zero = jnp.zeros_like(max_t)
    for i, v in enumerate((max_t, max_t, max_s, zero, sum_t, number, sum_s, zero)):
        total[i : i + 1] = v


def score(pooled, student, own_t, own_s, got):
    vmem = pl.BlockSpec(memory_space=pltpu.VMEM)
    anywhere = pl.BlockSpec(memory_space=pl.ANY)
    return pl.pallas_call(
        score_kernel,
        in_specs=[vmem, vmem] + [anywhere] * 8,
        out_specs=[vmem] * 4,
        out_shape=[
            jax.ShapeDtypeStruct((8 * PIECE, ROWS), F32),
            jax.ShapeDtypeStruct((8 * PIECE, ROWS), F32),
            jax.ShapeDtypeStruct((8 * PIECE, D_S), BF16),
            jax.ShapeDtypeStruct((8, ROWS), F32),
        ],
        scratch_shapes=[
            pltpu.VMEM((8 * PIECE, D_T), BF16),
            pltpu.SemaphoreType.DMA((14,)),
        ],
        compiler_params=pltpu.CompilerParams(vmem_limit_bytes=40 << 20),
        cost_estimate=pl.CostEstimate(
            flops=2 * 8 * PIECE * ROWS * (D_T + D_S), bytes_accessed=15 << 20, transcendentals=0
        ),
        name="score",
    )(pooled, student, own_t, own_s, *got)


def grad_kernel(exp_t, exp_s, mine, stats, prompts, grad, kl):
    every = stats[...]
    top = jnp.max(every, axis=0)
    weight = pltpu.roll(jnp.exp(every - top[None]), 4, 1)
    total = jnp.sum(every * weight, axis=0)
    top_t, top_s = top[0:1], top[2:3]
    sum_t, number, sum_s = total[4:5], total[5:6], total[6:7]
    kl[...] = number / sum_t - top_t - jnp.log(sum_t) + top_s + jnp.log(sum_s)
    scale_t = jnp.exp(mine[0:1] - top_t) / sum_t
    scale_s = jnp.exp(mine[2:3] - top_s) / sum_s
    difference = (exp_s[...] * scale_s - exp_t[...] * scale_t).astype(BF16)
    grad[...] = lax.dot_general(
        difference, prompts[...], CONTRACT_FIRST, preferred_element_type=F32
    )


def gradient(exp_t, exp_s, mine, stats, prompts):
    vmem = pl.BlockSpec(memory_space=pltpu.VMEM)
    return pl.pallas_call(
        grad_kernel,
        in_specs=[vmem] * 5,
        out_specs=[vmem] * 2,
        out_shape=[
            jax.ShapeDtypeStruct((ROWS, D_S), F32),
            jax.ShapeDtypeStruct((1, ROWS), F32),
        ],
        compiler_params=pltpu.CompilerParams(vmem_limit_bytes=40 << 20),
        cost_estimate=pl.CostEstimate(
            flops=2 * 8 * PIECE * ROWS * D_S, bytes_accessed=8 << 20, transcendentals=0
        ),
        name="gradient",
    )(exp_t, exp_s, mine, stats, prompts)


def body(teacher_maps, pool_index, pairing, teacher_prompts, student_patches, student_prompts):
    n_w, n_z = 8, 8
    xhi, zh, zl = (lax.axis_index(a) for a in ("xhi", "zh", "zl"))
    w = xhi * 4 + lax.axis_index("y")
    z = zh * 2 + zl

    core = lax.axis_index("core")
    half = jnp.concatenate(
        [
            lax.dynamic_slice_in_dim(teacher_prompts, core * PIECE, PIECE, 0),
            lax.dynamic_slice_in_dim(student_prompts, core * PIECE, PIECE, 0),
        ],
        axis=1,
    )
    flip2, flip4 = ([(i, n - 1 - i) for i in range(n)] for n in (2, 4))
    teacher_maps, half = lax.optimization_barrier((teacher_maps, half))
    got_x = lax.ppermute(half, ("xlo", "xhi"), flip4)
    got_z = lax.ppermute(half, "zl", flip2)

    patches = student_patches.reshape(4, 2, 4, 2, 16, D_S)
    patches = lax.dynamic_index_in_dim(patches, xhi, 1, keepdims=False)
    patches = lax.dynamic_index_in_dim(patches, zl, 2, keepdims=False)
    student_rows = patches.transpose(1, 0, 2, 3).reshape(ROWS, D_S)

    every_map = lax.all_gather(teacher_maps, IMG, axis=0, tiled=True)
    wanted = pairing[:, None] == jnp.arange(16)[None]
    owned = jnp.sum(jnp.where(wanted[:, :, None, None], every_map[None], 0), axis=1, dtype=BF16)
    pairs = [((v + 1) * n_z + c, v * n_z + c) for v in range(n_w - 1) for c in (0, 1)]
    pairs += [(v * n_z + c, (v + 1) * n_z + c) for v in range(n_w - 1) for c in (6, 7)]
    halo = lax.ppermute(owned, PRM, pairs)
    to_upper = jnp.where(z >= 6, halo, owned)
    to_lower = jnp.where(z <= 1, halo, owned)
    to_z = jnp.stack([to_upper, to_lower], axis=1).reshape((8,) + owned.shape[1:])
    to_z, got_x, got_z = lax.optimization_barrier((to_z, got_x, got_z))
    got_xz = lax.ppermute(got_z, ("xlo", "xhi"), flip4)
    cells = swap(to_z, Z)
    cells = cells.reshape(128, D_T)
    source = jnp.arange(8)
    grid_row = 4 * w + source // 2
    grid_row = jnp.where(
        zl == 0,
        jnp.where(source >= 6, 4 * w - 1, grid_row),
        jnp.where(source <= 1, 4 * w + 4, grid_row),
    )
    cell_id = grid_row[:, None] * 32 + (source % 2)[:, None] * 16 + jnp.arange(16)[None]
    cell_id = cell_id.reshape(-1)
    index = lax.dynamic_slice_in_dim(pool_index, 16 * (2 * w + zl), 16, 0)
    counts = jnp.sum((index[:, :, None] == cell_id[None, None, :]).astype(F32), axis=1)
    pooled = (jnp.dot(counts.astype(BF16), cells, preferred_element_type=F32) * 0.25).astype(BF16)

    pooled = spread(pooled, "zh", 4).reshape(64, D_T)
    pooled, got_xz = lax.optimization_barrier((pooled, got_xz))
    got = [got_x, got_z, got_xz]
    got += [lax.ppermute(piece, "core", flip2) for piece in got]
    pooled = spread(pooled, "y", 4).reshape(ROWS, D_T)

    exp_t, exp_s, prompts, total = score(
        pooled, student_rows, teacher_prompts, student_prompts, got
    )
    stats = spread(total, ("y", "zh"), 16)
    grad_term, kl_rows = gradient(exp_t, exp_s, total, stats, prompts)

    grad = jnp.sum(swap(grad_term.reshape(4, 64, D_S), "y"), axis=0)
    grad = jnp.sum(swap(grad.reshape(4, 16, D_S), "zh"), axis=0).astype(BF16)
    grad = spread(grad, Z, n_z)
    grad = spread(grad, ("xhi", "y"), n_w)
    patch_grad = grad.reshape(n_w, 4, 2, 16, D_S).transpose(1, 0, 2, 3, 4)

    kl_other = lax.ppermute(kl_rows, "zl", flip2)
    kl = jnp.where(zl == 0, jnp.stack([kl_rows, kl_other]), jnp.stack([kl_other, kl_rows]))
    kl_other = lax.ppermute(kl, "xhi", flip2)
    kl = jnp.where(xhi == 0, jnp.stack([kl, kl_other]), jnp.stack([kl_other, kl]))
    patch_kl = kl.reshape(2, 2, 4, 4, 16).transpose(3, 0, 2, 1, 4).reshape(4, -1)
    return patch_kl, patch_grad.reshape(student_patches.shape)


def solution(mesh):
    split = Mesh(mesh.devices.reshape(2, 2, 2, 4, 4, 2), IMG + PRM)
    placed = (
        P(IMG, PRM, None),
        P(),
        P(IMG),
        P(PRM, None),
        P(IMG, None, None),
        P(PRM, None),
    )
    return jax.shard_map(
        body,
        mesh=split,
        in_specs=placed,
        out_specs=(P(IMG, None), P(IMG, None, None)),
        check_vma=False,
    )
```

```python
import functools

import jax
import jax.numpy as jnp
from jax import lax
from jax.experimental import pallas as pl
from jax.experimental.pallas import tpu as pltpu
from jax.sharding import Mesh, PartitionSpec as P

IMG = ("xlo", "core")
PRM = ("xhi", "y", "zh", "zl")
Z = ("zh", "zl")
F32 = jnp.float32
BF16 = jnp.bfloat16
D_T = 1152
D_S = 768
PIECE = 256
ROWS = 256
CONTRACT_LAST = (((1,), (1,)), ((), ()))
CONTRACT_FIRST = (((0,), (0,)), ((), ()))


def swap(x, axis):
    return lax.all_to_all(x, axis, split_axis=0, concat_axis=0, tiled=True)


def spread(x, axis, size):
    return swap(jnp.broadcast_to(x[None], (size,) + x.shape), axis)


def exchange_sum(x, axis, starts):
    rows = x.shape[0] // 4
    total = lax.dynamic_slice_in_dim(x, starts[0], rows, 0, allow_negative_indices=False)
    for k in range(1, 4):
        part = lax.dynamic_slice_in_dim(x, starts[k], rows, 0, allow_negative_indices=False)
        total = total + lax.ppermute(part, axis, [(i, i ^ k) for i in range(4)])
    return total


def half_kernel(teacher, student, half, sems):
    rows = pl.ds(lax.axis_index("core") * PIECE, PIECE)
    copies = [
        pltpu.make_async_copy(teacher.at[rows], half.at[:, 0:D_T], sems.at[0]),
        pltpu.make_async_copy(student.at[rows], half.at[:, D_T : D_T + D_S], sems.at[1]),
    ]
    for c in copies:
        c.start()
    for c in copies:
        c.wait()


def core_half(teacher, student):
    hbm = pl.BlockSpec(memory_space=pltpu.HBM)
    return pl.pallas_call(
        half_kernel,
        in_specs=[hbm, hbm],
        out_specs=pl.BlockSpec(memory_space=pltpu.VMEM),
        out_shape=pltpu.VMEM((PIECE, D_T + D_S), BF16),
        scratch_shapes=[pltpu.SemaphoreType.DMA((2,))],
        name="half",
    )(teacher, student)


def score_kernel(pooled, student_rows, own_t, own_s, *refs):
    got, (exp_t, exp_s, prompts, total, student, teacher, sems) = refs[:6], refs[6:]
    copies = []

    def copy(source, target):
        copies.append(pltpu.make_async_copy(source, target, sems.at[len(copies)]))
        copies[-1].start()

    copy(own_t, teacher.at[0 : 2 * PIECE])
    copy(student_rows, student)
    copy(own_s, prompts.at[0 : 2 * PIECE])
    for i, piece in enumerate(got):
        at = (2 + i) * PIECE
        copy(piece.at[:, 0:D_T], teacher.at[at : at + PIECE])
        copy(piece.at[:, D_T : D_T + D_S], prompts.at[at : at + PIECE])

    spans = [(0, 2 * PIECE, copies[:3]), (2 * PIECE, 8 * PIECE, copies[3:])]
    logits = []
    for first, last, needed in spans:
        for c in needed:
            c.wait()
        logits.append(
            (
                lax.dot_general(
                    teacher[first:last], pooled[...], CONTRACT_LAST, preferred_element_type=F32
                ),
                lax.dot_general(
                    prompts[first:last], student[...], CONTRACT_LAST, preferred_element_type=F32
                ),
            )
        )
    max_t, max_s = (
        functools.reduce(jnp.maximum, [jnp.max(both[i], axis=0, keepdims=True) for both in logits])
        for i in range(2)
    )
    sum_t = number = sum_s = 0.0
    for (first, last, _), (logits_t, logits_s) in zip(spans, logits):
        e_t = jnp.exp(logits_t - max_t)
        e_s = jnp.exp(logits_s - max_s)
        exp_t[first:last] = e_t
        exp_s[first:last] = e_s
        sum_t += jnp.sum(e_t, axis=0, keepdims=True)
        number += jnp.sum(e_t * (logits_t - logits_s), axis=0, keepdims=True)
        sum_s += jnp.sum(e_s, axis=0, keepdims=True)
    zero = jnp.zeros_like(max_t)
    for i, v in enumerate((max_t, max_t, max_s, zero, sum_t, number, sum_s, zero)):
        total[i : i + 1] = v


def score(pooled, student, own_t, own_s, got):
    vmem = pl.BlockSpec(memory_space=pltpu.VMEM)
    hbm = pl.BlockSpec(memory_space=pltpu.HBM)
    in_hbm = [
        pltpu.with_memory_space_constraint(x, pltpu.HBM) for x in (student, own_t, own_s, *got)
    ]
    return pl.pallas_call(
        score_kernel,
        in_specs=[vmem] + [hbm] * 9,
        out_specs=[vmem] * 4,
        out_shape=[
            jax.ShapeDtypeStruct((8 * PIECE, ROWS), F32),
            jax.ShapeDtypeStruct((8 * PIECE, ROWS), F32),
            jax.ShapeDtypeStruct((8 * PIECE, D_S), BF16),
            jax.ShapeDtypeStruct((8, ROWS), F32),
        ],
        scratch_shapes=[
            pltpu.VMEM((ROWS, D_S), BF16),
            pltpu.VMEM((8 * PIECE, D_T), BF16),
            pltpu.SemaphoreType.DMA((15,)),
        ],
        compiler_params=pltpu.CompilerParams(vmem_limit_bytes=24 << 20),
        cost_estimate=pl.CostEstimate(
            flops=2 * 8 * PIECE * ROWS * (D_T + D_S), bytes_accessed=15 << 20, transcendentals=0
        ),
        name="score",
    )(pooled, *in_hbm)


def grad_kernel(exp_t, exp_s, mine, stats, prompts, grad, kl):
    every = stats[...]
    top = jnp.max(every, axis=0)
    weight = pltpu.roll(jnp.exp(every - top[None]), 4, 1)
    total = jnp.sum(every * weight, axis=0)
    top_t, top_s = top[0:1], top[2:3]
    sum_t, number, sum_s = total[4:5], total[5:6], total[6:7]
    kl[...] = number / sum_t - top_t - jnp.log(sum_t) + top_s + jnp.log(sum_s)
    scale_t = jnp.exp(mine[0:1] - top_t) / sum_t
    scale_s = jnp.exp(mine[2:3] - top_s) / sum_s
    difference = (exp_s[...] * scale_s - exp_t[...] * scale_t).astype(BF16)
    grad[...] = lax.dot_general(
        difference, prompts[...], CONTRACT_FIRST, preferred_element_type=F32
    )


def gradient(exp_t, exp_s, mine, stats, prompts):
    vmem = pl.BlockSpec(memory_space=pltpu.VMEM)
    return pl.pallas_call(
        grad_kernel,
        in_specs=[vmem] * 5,
        out_specs=[vmem] * 2,
        out_shape=[
            jax.ShapeDtypeStruct((ROWS, D_S), F32),
            jax.ShapeDtypeStruct((1, ROWS), F32),
        ],
        compiler_params=pltpu.CompilerParams(vmem_limit_bytes=24 << 20),
        cost_estimate=pl.CostEstimate(
            flops=2 * 8 * PIECE * ROWS * D_S, bytes_accessed=8 << 20, transcendentals=0
        ),
        name="gradient",
    )(exp_t, exp_s, mine, stats, prompts)


def body(teacher_maps, pool_index, pairing, teacher_prompts, student_patches, student_prompts):
    n_w, n_z = 8, 8
    xhi, y, zh, zl = (lax.axis_index(a) for a in PRM)
    w = xhi * 4 + y
    z = zh * 2 + zl

    half = core_half(teacher_prompts, student_prompts)
    flip2, flip4 = ([(i, n - 1 - i) for i in range(n)] for n in (2, 4))
    teacher_maps, half = lax.optimization_barrier((teacher_maps, half))
    got_z = lax.ppermute(half, "zl", flip2)
    got_x = lax.ppermute(half, ("xlo", "xhi"), flip4)

    patches = student_patches.reshape(4, 2, 4, 2, 16, D_S)
    patches = lax.dynamic_index_in_dim(patches, xhi, 1, keepdims=False)
    patches = lax.dynamic_index_in_dim(patches, zl, 2, keepdims=False)
    student_rows = patches.transpose(1, 0, 2, 3).reshape(ROWS, D_S)

    source = jnp.arange(8)
    grid_row = 4 * w + source // 2
    grid_row = jnp.where(
        zl == 0,
        jnp.where(source >= 6, 4 * w - 1, grid_row),
        jnp.where(source <= 1, 4 * w + 4, grid_row),
    )
    cell_id = grid_row[:, None] * 32 + (source % 2)[:, None] * 16 + jnp.arange(16)[None]
    cell_id = cell_id.reshape(-1)
    index = lax.dynamic_slice_in_dim(pool_index, 16 * (2 * w + zl), 16, 0)
    counts = jnp.sum((index[:, :, None] == cell_id[None, None, :]).astype(F32), axis=1).astype(BF16)
    starts_y = [(y ^ k) * 64 for k in range(4)]
    starts_z = [(zh ^ k) * 16 for k in range(4)]

    every_map = lax.all_gather(teacher_maps, IMG, axis=0, tiled=True)
    wanted = pairing[:, None] == jnp.arange(16)[None]
    owned = jnp.sum(jnp.where(wanted[:, :, None, None], every_map[None], 0), axis=1, dtype=BF16)
    pairs = [((v + 1) * n_z + c, v * n_z + c) for v in range(n_w - 1) for c in (0, 1)]
    pairs += [(v * n_z + c, (v + 1) * n_z + c) for v in range(n_w - 1) for c in (6, 7)]
    halo = lax.ppermute(owned, PRM, pairs)
    lower = jnp.arange(2)[None, :, None, None] == 1
    outside = jnp.where(lower, z <= 1, z >= 6)
    to_z = jnp.where(outside, halo[:, None], owned[:, None]).reshape((8,) + owned.shape[1:])
    to_z, got_z, counts, starts_y, starts_z = lax.optimization_barrier(
        (to_z, got_z, counts, starts_y, starts_z)
    )
    got_xz = lax.ppermute(got_z, ("xlo", "xhi"), flip4)
    cells = swap(to_z, Z)
    cells = cells.reshape(128, D_T)
    pooled = (jnp.dot(counts, cells, preferred_element_type=F32) * 0.25).astype(BF16)

    pooled, got_x = lax.optimization_barrier((pooled, got_x))
    got = [got_x, got_z, got_xz]
    got += [lax.ppermute(piece, "core", flip2) for piece in got]
    pooled = spread(pooled, ("y", "zh"), 16).reshape(ROWS, D_T)

    exp_t, exp_s, prompts, total = score(pooled, student_rows, teacher_prompts, student_prompts, got)
    stats = spread(total, ("y", "zh"), 16)
    grad_term, kl_rows = gradient(exp_t, exp_s, total, stats, prompts)

    place = kl_rows.reshape(4, 4, 16).transpose(1, 0, 2)[:, None, :, None, :]
    mine = (jnp.arange(2)[:, None] == xhi) & (jnp.arange(2)[None] == zl)
    place = jnp.where(mine[None, :, None, :, None], place, 0.0).reshape(4, 256)

    grad = exchange_sum(grad_term, "y", starts_y)
    grad = exchange_sum(grad, "zh", starts_z).astype(BF16)
    grad = spread(grad, Z, n_z)
    grad, place = lax.optimization_barrier((grad, place))
    grad = spread(grad, ("xhi", "y"), n_w)
    patch_grad = grad.reshape(n_w, 4, 2, 16, D_S).transpose(1, 0, 2, 3, 4)

    patch_kl = (
        (place + lax.ppermute(place, "zl", flip2))
        + lax.ppermute(place, "xhi", flip2)
        + lax.ppermute(place, ("xhi", "zl"), flip4)
    )
    return patch_kl, patch_grad.reshape(student_patches.shape)


def solution(mesh):
    split = Mesh(mesh.devices.reshape(2, 2, 2, 4, 4, 2), IMG + PRM)
    placed = (
        P(IMG, PRM, None),
        P(),
        P(IMG),
        P(PRM, None),
        P(IMG, None, None),
        P(PRM, None),
    )
    return jax.shard_map(
        body,
        mesh=split,
        in_specs=placed,
        out_specs=(P(IMG, None), P(IMG, None, None)),
        check_vma=False,
    )
```

```python
import functools

import jax
import jax.numpy as jnp
from jax import lax
from jax.experimental import pallas as pl
from jax.experimental.pallas import tpu as pltpu
from jax.sharding import Mesh, PartitionSpec as P

IMG = ("xlo", "core")
PRM = ("xhi", "y", "zh", "zl")
Z = ("zh", "zl")
F32 = jnp.float32
BF16 = jnp.bfloat16
D_T = 1152
D_S = 768
PIECE = 256
ROWS = 256
CONTRACT_LAST = (((1,), (1,)), ((), ()))
CONTRACT_FIRST = (((0,), (0,)), ((), ()))


def swap(x, axis):
    return lax.all_to_all(x, axis, split_axis=0, concat_axis=0, tiled=True)


def spread(x, axis, size):
    return swap(jnp.broadcast_to(x[None], (size,) + x.shape), axis)


def exchange_sum(x, axis, starts):
    rows = x.shape[0] // 4
    total = lax.dynamic_slice_in_dim(x, starts[0], rows, 0, allow_negative_indices=False)
    for k in range(1, 4):
        part = lax.dynamic_slice_in_dim(x, starts[k], rows, 0, allow_negative_indices=False)
        total = total + lax.ppermute(part, axis, [(i, i ^ k) for i in range(4)])
    return total


def half_kernel(teacher, student, half, sems):
    rows = pl.ds(lax.axis_index("core") * PIECE, PIECE)
    copies = [
        pltpu.make_async_copy(teacher.at[rows], half.at[:, 0:D_T], sems.at[0]),
        pltpu.make_async_copy(student.at[rows], half.at[:, D_T : D_T + D_S], sems.at[1]),
    ]
    for c in copies:
        c.start()
    for c in copies:
        c.wait()


def core_half(teacher, student):
    hbm = pl.BlockSpec(memory_space=pltpu.HBM)
    return pl.pallas_call(
        half_kernel,
        in_specs=[hbm, hbm],
        out_specs=pl.BlockSpec(memory_space=pltpu.VMEM),
        out_shape=pltpu.VMEM((PIECE, D_T + D_S), BF16),
        scratch_shapes=[pltpu.SemaphoreType.DMA((2,))],
        name="half",
    )(teacher, student)


def student_kernel(student_rows, own_s, *refs):
    got, (out_l, out_e, total, student, prompts, logits, exps, sems) = refs[:6], refs[6:]
    copies = [
        pltpu.make_async_copy(student_rows, student, sems.at[0]),
        pltpu.make_async_copy(own_s, prompts.at[0 : 2 * PIECE], sems.at[1]),
    ]
    for i, piece in enumerate(got):
        at = (2 + i) * PIECE
        copies.append(
            pltpu.make_async_copy(
                piece.at[:, D_T : D_T + D_S], prompts.at[at : at + PIECE], sems.at[2 + i]
            )
        )
    for c in copies:
        c.start()
    for c in copies:
        c.wait()
    scores = lax.dot_general(
        prompts[...], student[...], CONTRACT_LAST, preferred_element_type=F32
    )
    logits[...] = scores
    out = [pltpu.make_async_copy(logits, out_l, sems.at[8])]
    out[0].start()
    top = jnp.max(scores, axis=0, keepdims=True)
    e = jnp.exp(scores - top)
    exps[...] = e
    out.append(pltpu.make_async_copy(exps, out_e, sems.at[9]))
    out[1].start()
    zero = jnp.zeros_like(top)
    for i, v in enumerate((top, jnp.sum(e, axis=0, keepdims=True)) + (zero,) * 6):
        total[i : i + 1] = v
    for c in out:
        c.wait()


def student_score(student, own_s, got):
    hbm = pl.BlockSpec(memory_space=pltpu.HBM)
    in_hbm = [pltpu.with_memory_space_constraint(x, pltpu.HBM) for x in (student, own_s, *got)]
    return pl.pallas_call(
        student_kernel,
        in_specs=[hbm] * 8,
        out_specs=[hbm, hbm, pl.BlockSpec(memory_space=pltpu.VMEM)],
        out_shape=[
            pltpu.HBM((8 * PIECE, ROWS), F32),
            pltpu.HBM((8 * PIECE, ROWS), F32),
            jax.ShapeDtypeStruct((8, ROWS), F32),
        ],
        scratch_shapes=[
            pltpu.VMEM((ROWS, D_S), BF16),
            pltpu.VMEM((8 * PIECE, D_S), BF16),
            pltpu.VMEM((8 * PIECE, ROWS), F32),
            pltpu.VMEM((8 * PIECE, ROWS), F32),
            pltpu.SemaphoreType.DMA((10,)),
        ],
        compiler_params=pltpu.CompilerParams(vmem_limit_bytes=24 << 20),
        cost_estimate=pl.CostEstimate(
            flops=2 * 8 * PIECE * ROWS * D_S, bytes_accessed=8 << 20, transcendentals=0
        ),
        name="student",
    )(*in_hbm)


def teacher_kernel(pooled, total_s, own_t, scores_s, in_exp, own_s, *refs):
    got, (exp_t, exp_s, prompts, total, teacher, student, sems) = refs[:6], refs[6:]
    copies = []

    def copy(source, target):
        copies.append(pltpu.make_async_copy(source, target, sems.at[len(copies)]))
        copies[-1].start()

    copy(own_t, teacher.at[0 : 2 * PIECE])
    for i, piece in enumerate(got):
        at = (2 + i) * PIECE
        copy(piece.at[:, 0:D_T], teacher.at[at : at + PIECE])
    copy(scores_s, student)
    copy(in_exp, exp_s)
    copy(own_s, prompts.at[0 : 2 * PIECE])
    for i, piece in enumerate(got):
        at = (2 + i) * PIECE
        copy(piece.at[:, D_T : D_T + D_S], prompts.at[at : at + PIECE])

    spans = [(0, 2 * PIECE, copies[:1]), (2 * PIECE, 8 * PIECE, copies[1:7])]
    logits = []
    for first, last, needed in spans:
        for c in needed:
            c.wait()
        logits.append(
            lax.dot_general(
                teacher[first:last], pooled[...], CONTRACT_LAST, preferred_element_type=F32
            )
        )
    max_t = functools.reduce(jnp.maximum, [jnp.max(x, axis=0, keepdims=True) for x in logits])
    copies[7].wait()
    sum_t = number = 0.0
    for (first, last, _), scores in zip(spans, logits):
        e_t = jnp.exp(scores - max_t)
        exp_t[first:last] = e_t
        sum_t += jnp.sum(e_t, axis=0, keepdims=True)
        number += jnp.sum(e_t * (scores - student[first:last]), axis=0, keepdims=True)
    zero = jnp.zeros_like(max_t)
    max_s, sum_s = total_s[0:1], total_s[1:2]
    for i, v in enumerate((max_t, max_t, max_s, zero, sum_t, number, sum_s, zero)):
        total[i : i + 1] = v
    for c in copies[8:]:
        c.wait()


def teacher_score(pooled, scores_s, exp_s, total_s, own_t, own_s, got):
    vmem = pl.BlockSpec(memory_space=pltpu.VMEM)
    hbm = pl.BlockSpec(memory_space=pltpu.HBM)
    in_hbm = [
        pltpu.with_memory_space_constraint(x, pltpu.HBM)
        for x in (own_t, scores_s, exp_s, own_s, *got)
    ]
    return pl.pallas_call(
        teacher_kernel,
        in_specs=[vmem, vmem] + [hbm] * 10,
        out_specs=[vmem] * 4,
        out_shape=[
            jax.ShapeDtypeStruct((8 * PIECE, ROWS), F32),
            jax.ShapeDtypeStruct((8 * PIECE, ROWS), F32),
            jax.ShapeDtypeStruct((8 * PIECE, D_S), BF16),
            jax.ShapeDtypeStruct((8, ROWS), F32),
        ],
        scratch_shapes=[
            pltpu.VMEM((8 * PIECE, D_T), BF16),
            pltpu.VMEM((8 * PIECE, ROWS), F32),
            pltpu.SemaphoreType.DMA((16,)),
        ],
        compiler_params=pltpu.CompilerParams(vmem_limit_bytes=24 << 20),
        cost_estimate=pl.CostEstimate(
            flops=2 * 8 * PIECE * ROWS * D_T, bytes_accessed=15 << 20, transcendentals=0
        ),
        name="teacher",
    )(pooled, total_s, *in_hbm)


def grad_kernel(exp_t, exp_s, mine, stats, prompts, grad, kl):
    every = stats[...]
    top = jnp.max(every, axis=0)
    weight = pltpu.roll(jnp.exp(every - top[None]), 4, 1)
    total = jnp.sum(every * weight, axis=0)
    top_t, top_s = top[0:1], top[2:3]
    sum_t, number, sum_s = total[4:5], total[5:6], total[6:7]
    kl[...] = number / sum_t - top_t - jnp.log(sum_t) + top_s + jnp.log(sum_s)
    scale_t = jnp.exp(mine[0:1] - top_t) / sum_t
    scale_s = jnp.exp(mine[2:3] - top_s) / sum_s
    difference = (exp_s[...] * scale_s - exp_t[...] * scale_t).astype(BF16)
    grad[...] = lax.dot_general(
        difference, prompts[...], CONTRACT_FIRST, preferred_element_type=F32
    )


def gradient(exp_t, exp_s, mine, stats, prompts):
    vmem = pl.BlockSpec(memory_space=pltpu.VMEM)
    return pl.pallas_call(
        grad_kernel,
        in_specs=[vmem] * 5,
        out_specs=[vmem] * 2,
        out_shape=[
            jax.ShapeDtypeStruct((ROWS, D_S), F32),
            jax.ShapeDtypeStruct((1, ROWS), F32),
        ],
        compiler_params=pltpu.CompilerParams(vmem_limit_bytes=24 << 20),
        cost_estimate=pl.CostEstimate(
            flops=2 * 8 * PIECE * ROWS * D_S, bytes_accessed=8 << 20, transcendentals=0
        ),
        name="gradient",
    )(exp_t, exp_s, mine, stats, prompts)


def body(teacher_maps, pool_index, pairing, teacher_prompts, student_patches, student_prompts):
    n_w, n_z = 8, 8
    xhi, y, zh, zl = (lax.axis_index(a) for a in PRM)
    w = xhi * 4 + y
    z = zh * 2 + zl

    half = core_half(teacher_prompts, student_prompts)
    flip2, flip4 = ([(i, n - 1 - i) for i in range(n)] for n in (2, 4))
    teacher_maps, half = lax.optimization_barrier((teacher_maps, half))
    got_z = lax.ppermute(half, "zl", flip2)
    got_x = lax.ppermute(half, ("xlo", "xhi"), flip4)

    patches = student_patches.reshape(4, 2, 4, 2, 16, D_S)
    patches = lax.dynamic_index_in_dim(patches, xhi, 1, keepdims=False)
    patches = lax.dynamic_index_in_dim(patches, zl, 2, keepdims=False)
    student_rows = patches.transpose(1, 0, 2, 3).reshape(ROWS, D_S)

    source = jnp.arange(8)
    grid_row = 4 * w + source // 2
    grid_row = jnp.where(
        zl == 0,
        jnp.where(source >= 6, 4 * w - 1, grid_row),
        jnp.where(source <= 1, 4 * w + 4, grid_row),
    )
    cell_id = grid_row[:, None] * 32 + (source % 2)[:, None] * 16 + jnp.arange(16)[None]
    cell_id = cell_id.reshape(-1)
    index = lax.dynamic_slice_in_dim(pool_index, 16 * (2 * w + zl), 16, 0)
    counts = jnp.sum((index[:, :, None] == cell_id[None, None, :]).astype(F32), axis=1).astype(BF16)
    mine = (jnp.arange(2)[:, None] == xhi) & (jnp.arange(2)[None] == zl)
    mine = jnp.broadcast_to(mine[None, :, None, :, None], (4, 2, 4, 2, 16))
    starts_y = [(y ^ k) * 64 for k in range(4)]
    starts_z = [(zh ^ k) * 16 for k in range(4)]

    every_map = lax.all_gather(teacher_maps, IMG, axis=0, tiled=True)
    wanted = pairing[:, None] == jnp.arange(16)[None]
    owned = jnp.sum(jnp.where(wanted[:, :, None, None], every_map[None], 0), axis=1, dtype=BF16)
    pairs = [((v + 1) * n_z + c, v * n_z + c) for v in range(n_w - 1) for c in (0, 1)]
    pairs += [(v * n_z + c, (v + 1) * n_z + c) for v in range(n_w - 1) for c in (6, 7)]
    halo = lax.ppermute(owned, PRM, pairs)
    lower = jnp.arange(2)[None, :, None, None] == 1
    outside = jnp.where(lower, z <= 1, z >= 6)
    to_z = jnp.where(outside, halo[:, None], owned[:, None]).reshape((8,) + owned.shape[1:])
    to_z, got_z, counts, mine, starts_y, starts_z = lax.optimization_barrier(
        (to_z, got_z, counts, mine, starts_y, starts_z)
    )
    got_xz = lax.ppermute(got_z, ("xlo", "xhi"), flip4)
    cells = swap(to_z, Z)
    cells = cells.reshape(128, D_T)
    pooled = (jnp.dot(counts, cells, preferred_element_type=F32) * 0.25).astype(BF16)

    pooled, got_x = lax.optimization_barrier((pooled, got_x))
    got = [got_x, got_z, got_xz]
    got += [lax.ppermute(piece, "core", flip2) for piece in got]
    scores_s, exp_s, total_s = student_score(student_rows, student_prompts, got)
    pooled = spread(pooled, ("y", "zh"), 16).reshape(ROWS, D_T)

    exp_t, exp_s, prompts, total = teacher_score(
        pooled, scores_s, exp_s, total_s, teacher_prompts, student_prompts, got
    )
    stats = spread(total, ("y", "zh"), 16)
    grad_term, kl_rows = gradient(exp_t, exp_s, total, stats, prompts)

    place = kl_rows.reshape(4, 4, 16).transpose(1, 0, 2)[:, None, :, None, :]
    place = jnp.where(mine, place, 0.0).reshape(4, 256)

    grad = exchange_sum(grad_term, "y", starts_y)
    others = [
        lax.ppermute(place, "zl", flip2),
        lax.ppermute(place, "xhi", flip2),
        lax.ppermute(place, ("xhi", "zl"), flip4),
    ]
    grad = exchange_sum(grad, "zh", starts_z).astype(BF16)
    patch_kl = ((place + others[0]) + others[1]) + others[2]
    grad, patch_kl = lax.optimization_barrier((grad, patch_kl))
    grad = spread(grad, Z, n_z)
    grad = spread(grad, ("xhi", "y"), n_w)
    patch_grad = grad.reshape(n_w, 4, 2, 16, D_S).transpose(1, 0, 2, 3, 4)

    return patch_kl, patch_grad.reshape(student_patches.shape)


def solution(mesh):
    split = Mesh(mesh.devices.reshape(2, 2, 2, 4, 4, 2), IMG + PRM)
    placed = (
        P(IMG, PRM, None),
        P(),
        P(IMG),
        P(PRM, None),
        P(IMG, None, None),
        P(PRM, None),
    )
    return jax.shard_map(
        body,
        mesh=split,
        in_specs=placed,
        out_specs=(P(IMG, None), P(IMG, None, None)),
        check_vma=False,
    )
```

```python
import functools

import jax
import jax.numpy as jnp
from jax import lax
from jax.experimental import pallas as pl
from jax.experimental.pallas import tpu as pltpu
from jax.sharding import Mesh, PartitionSpec as P

IMG = ("xlo", "core")
PRM = ("xhi", "y", "zh", "zl")
Z = ("zh", "zl")
F32 = jnp.float32
BF16 = jnp.bfloat16
D_T = 1152
D_S = 768
PIECE = 256
ROWS = 256
CONTRACT_LAST = (((1,), (1,)), ((), ()))
CONTRACT_FIRST = (((0,), (0,)), ((), ()))


def swap(x, axis):
    return lax.all_to_all(x, axis, split_axis=0, concat_axis=0, tiled=True)


def spread(x, axis, size):
    return swap(jnp.broadcast_to(x[None], (size,) + x.shape), axis)


def exchange_sum(x, axis, starts):
    rows = x.shape[0] // 4
    total = lax.dynamic_slice_in_dim(x, starts[0], rows, 0, allow_negative_indices=False)
    for k in range(1, 4):
        part = lax.dynamic_slice_in_dim(x, starts[k], rows, 0, allow_negative_indices=False)
        total = total + lax.ppermute(part, axis, [(i, i ^ k) for i in range(4)])
    return total


def half_kernel(teacher, student, half, sems):
    rows = pl.ds(lax.axis_index("core") * PIECE, PIECE)
    copies = [
        pltpu.make_async_copy(teacher.at[rows], half.at[:, 0:D_T], sems.at[0]),
        pltpu.make_async_copy(student.at[rows], half.at[:, D_T : D_T + D_S], sems.at[1]),
    ]
    for c in copies:
        c.start()
    for c in copies:
        c.wait()


def core_half(teacher, student):
    hbm = pl.BlockSpec(memory_space=pltpu.HBM)
    return pl.pallas_call(
        half_kernel,
        in_specs=[hbm, hbm],
        out_specs=pl.BlockSpec(memory_space=pltpu.VMEM),
        out_shape=pltpu.VMEM((PIECE, D_T + D_S), BF16),
        scratch_shapes=[pltpu.SemaphoreType.DMA((2,))],
        name="half",
    )(teacher, student)


def student_kernel(student_rows, own_s, *refs):
    got, (out_l, out_e, total, student, prompts, logits, exps, sems) = refs[:6], refs[6:]
    copies = [
        pltpu.make_async_copy(student_rows, student, sems.at[0]),
        pltpu.make_async_copy(own_s, prompts.at[0 : 2 * PIECE], sems.at[1]),
    ]
    for i, piece in enumerate(got):
        at = (2 + i) * PIECE
        copies.append(
            pltpu.make_async_copy(
                piece.at[:, D_T : D_T + D_S], prompts.at[at : at + PIECE], sems.at[2 + i]
            )
        )
    for c in copies:
        c.start()
    for c in copies:
        c.wait()
    scores = lax.dot_general(
        prompts[...], student[...], CONTRACT_LAST, preferred_element_type=F32
    )
    logits[...] = scores
    out = [pltpu.make_async_copy(logits, out_l, sems.at[8])]
    out[0].start()
    top = jnp.max(scores, axis=0, keepdims=True)
    e = jnp.exp(scores - top)
    exps[...] = e
    out.append(pltpu.make_async_copy(exps, out_e, sems.at[9]))
    out[1].start()
    zero = jnp.zeros_like(top)
    for i, v in enumerate((top, jnp.sum(e, axis=0, keepdims=True)) + (zero,) * 6):
        total[i : i + 1] = v
    for c in out:
        c.wait()


def student_score(student, own_s, got):
    hbm = pl.BlockSpec(memory_space=pltpu.HBM)
    in_hbm = [pltpu.with_memory_space_constraint(x, pltpu.HBM) for x in (student, own_s, *got)]
    return pl.pallas_call(
        student_kernel,
        in_specs=[hbm] * 8,
        out_specs=[hbm, hbm, pl.BlockSpec(memory_space=pltpu.VMEM)],
        out_shape=[
            pltpu.HBM((8 * PIECE, ROWS), F32),
            pltpu.HBM((8 * PIECE, ROWS), F32),
            jax.ShapeDtypeStruct((8, ROWS), F32),
        ],
        scratch_shapes=[
            pltpu.VMEM((ROWS, D_S), BF16),
            pltpu.VMEM((8 * PIECE, D_S), BF16),
            pltpu.VMEM((8 * PIECE, ROWS), F32),
            pltpu.VMEM((8 * PIECE, ROWS), F32),
            pltpu.SemaphoreType.DMA((10,)),
        ],
        compiler_params=pltpu.CompilerParams(vmem_limit_bytes=24 << 20),
        cost_estimate=pl.CostEstimate(
            flops=2 * 8 * PIECE * ROWS * D_S, bytes_accessed=8 << 20, transcendentals=0
        ),
        name="student",
    )(*in_hbm)


def teacher_kernel(pooled, total_s, own_t, scores_s, in_exp, own_s, *refs):
    got, (exp_t, exp_s, prompts, total, teacher, student, sems) = refs[:6], refs[6:]
    copies = []

    def copy(source, target):
        copies.append(pltpu.make_async_copy(source, target, sems.at[len(copies)]))
        copies[-1].start()

    copy(own_t, teacher.at[0 : 2 * PIECE])
    for i, piece in enumerate(got):
        at = (2 + i) * PIECE
        copy(piece.at[:, 0:D_T], teacher.at[at : at + PIECE])
    copy(scores_s, student)
    copy(in_exp, exp_s)
    copy(own_s, prompts.at[0 : 2 * PIECE])
    for i, piece in enumerate(got):
        at = (2 + i) * PIECE
        copy(piece.at[:, D_T : D_T + D_S], prompts.at[at : at + PIECE])

    spans = [(0, 2 * PIECE, copies[:1]), (2 * PIECE, 8 * PIECE, copies[1:7])]
    logits = []
    for first, last, needed in spans:
        for c in needed:
            c.wait()
        logits.append(
            lax.dot_general(
                teacher[first:last], pooled[...], CONTRACT_LAST, preferred_element_type=F32
            )
        )
    max_t = functools.reduce(jnp.maximum, [jnp.max(x, axis=0, keepdims=True) for x in logits])
    copies[7].wait()
    sum_t = number = 0.0
    for (first, last, _), scores in zip(spans, logits):
        e_t = jnp.exp(scores - max_t)
        exp_t[first:last] = e_t
        sum_t += jnp.sum(e_t, axis=0, keepdims=True)
        number += jnp.sum(e_t * (scores - student[first:last]), axis=0, keepdims=True)
    zero = jnp.zeros_like(max_t)
    max_s, sum_s = total_s[0:1], total_s[1:2]
    for i, v in enumerate((max_t, max_t, max_s, zero, sum_t, number, sum_s, zero)):
        total[i : i + 1] = v
    for c in copies[8:]:
        c.wait()


def teacher_score(pooled, scores_s, exp_s, total_s, own_t, own_s, got):
    vmem = pl.BlockSpec(memory_space=pltpu.VMEM)
    hbm = pl.BlockSpec(memory_space=pltpu.HBM)
    in_hbm = [
        pltpu.with_memory_space_constraint(x, pltpu.HBM)
        for x in (own_t, scores_s, exp_s, own_s, *got)
    ]
    return pl.pallas_call(
        teacher_kernel,
        in_specs=[vmem, vmem] + [hbm] * 10,
        out_specs=[vmem] * 4,
        out_shape=[
            jax.ShapeDtypeStruct((8 * PIECE, ROWS), F32),
            jax.ShapeDtypeStruct((8 * PIECE, ROWS), F32),
            jax.ShapeDtypeStruct((8 * PIECE, D_S), BF16),
            jax.ShapeDtypeStruct((8, ROWS), F32),
        ],
        scratch_shapes=[
            pltpu.VMEM((8 * PIECE, D_T), BF16),
            pltpu.VMEM((8 * PIECE, ROWS), F32),
            pltpu.SemaphoreType.DMA((16,)),
        ],
        compiler_params=pltpu.CompilerParams(vmem_limit_bytes=24 << 20),
        cost_estimate=pl.CostEstimate(
            flops=2 * 8 * PIECE * ROWS * D_T, bytes_accessed=15 << 20, transcendentals=0
        ),
        name="teacher",
    )(pooled, total_s, *in_hbm)


def grad_kernel(exp_t, exp_s, mine, stats, prompts, grad, kl):
    every = stats[...]
    top = jnp.max(every, axis=0)
    weight = pltpu.roll(jnp.exp(every - top[None]), 4, 1)
    total = jnp.sum(every * weight, axis=0)
    top_t, top_s = top[0:1], top[2:3]
    sum_t, number, sum_s = total[4:5], total[5:6], total[6:7]
    rows = number / sum_t - top_t - jnp.log(sum_t) + top_s + jnp.log(sum_s)
    rows = jnp.broadcast_to(rows, (8, ROWS))
    image = lax.broadcasted_iota(jnp.int32, rows.shape, 0)
    lane = lax.broadcasted_iota(jnp.int32, rows.shape, 1)
    placed = jnp.zeros_like(rows)
    for i in range(4):
        for y in range(4):
            moved = pltpu.roll(rows, (32 * y - 64 * y - 16 * i) % ROWS, 1)
            here = (image == i) & (lane >= 32 * y) & (lane < 32 * y + 16)
            placed = jnp.where(here, moved, placed)
    first = lax.axis_index("xhi") * 128 + lax.axis_index("zl") * 16
    kl[...] = pltpu.roll(placed, first, 1)[0:4]
    scale_t = jnp.exp(mine[0:1] - top_t) / sum_t
    scale_s = jnp.exp(mine[2:3] - top_s) / sum_s
    difference = (exp_s[...] * scale_s - exp_t[...] * scale_t).astype(BF16)
    grad[...] = lax.dot_general(
        difference, prompts[...], CONTRACT_FIRST, preferred_element_type=F32
    )


def gradient(exp_t, exp_s, mine, stats, prompts):
    vmem = pl.BlockSpec(memory_space=pltpu.VMEM)
    return pl.pallas_call(
        grad_kernel,
        in_specs=[vmem] * 5,
        out_specs=[vmem] * 2,
        out_shape=[
            jax.ShapeDtypeStruct((ROWS, D_S), F32),
            jax.ShapeDtypeStruct((4, ROWS), F32),
        ],
        compiler_params=pltpu.CompilerParams(vmem_limit_bytes=24 << 20),
        cost_estimate=pl.CostEstimate(
            flops=2 * 8 * PIECE * ROWS * D_S, bytes_accessed=8 << 20, transcendentals=0
        ),
        name="gradient",
    )(exp_t, exp_s, mine, stats, prompts)


def body(teacher_maps, pool_index, pairing, teacher_prompts, student_patches, student_prompts):
    n_w, n_z = 8, 8
    xhi, y, zh, zl = (lax.axis_index(a) for a in PRM)
    w = xhi * 4 + y
    z = zh * 2 + zl

    half = core_half(teacher_prompts, student_prompts)
    flip2, flip4 = ([(i, n - 1 - i) for i in range(n)] for n in (2, 4))
    teacher_maps, half = lax.optimization_barrier((teacher_maps, half))
    got_z = lax.ppermute(half, "zl", flip2)
    got_x = lax.ppermute(half, ("xlo", "xhi"), flip4)

    patches = student_patches.reshape(4, 2, 4, 2, 16, D_S)
    patches = lax.dynamic_index_in_dim(patches, xhi, 1, keepdims=False)
    patches = lax.dynamic_index_in_dim(patches, zl, 2, keepdims=False)
    student_rows = patches.transpose(1, 0, 2, 3).reshape(ROWS, D_S)

    source = jnp.arange(8)
    grid_row = 4 * w + source // 2
    grid_row = jnp.where(
        zl == 0,
        jnp.where(source >= 6, 4 * w - 1, grid_row),
        jnp.where(source <= 1, 4 * w + 4, grid_row),
    )
    cell_id = grid_row[:, None] * 32 + (source % 2)[:, None] * 16 + jnp.arange(16)[None]
    cell_id = cell_id.reshape(-1)
    index = lax.dynamic_slice_in_dim(pool_index, 16 * (2 * w + zl), 16, 0)
    counts = jnp.sum((index[:, :, None] == cell_id[None, None, :]).astype(F32), axis=1).astype(BF16)
    starts_y = [(y ^ k) * 64 for k in range(4)]
    starts_z = [(zh ^ k) * 16 for k in range(4)]

    every_map = lax.all_gather(teacher_maps, IMG, axis=0, tiled=True)
    wanted = pairing[:, None] == jnp.arange(16)[None]
    owned = jnp.sum(jnp.where(wanted[:, :, None, None], every_map[None], 0), axis=1, dtype=BF16)
    pairs = [((v + 1) * n_z + c, v * n_z + c) for v in range(n_w - 1) for c in (0, 1)]
    pairs += [(v * n_z + c, (v + 1) * n_z + c) for v in range(n_w - 1) for c in (6, 7)]
    halo = lax.ppermute(owned, PRM, pairs)
    lower = jnp.arange(2)[None, :, None, None] == 1
    outside = jnp.where(lower, z <= 1, z >= 6)
    to_z = jnp.where(outside, halo[:, None], owned[:, None]).reshape((8,) + owned.shape[1:])
    to_z, got_z, counts, starts_y, starts_z = lax.optimization_barrier(
        (to_z, got_z, counts, starts_y, starts_z)
    )
    got_xz = lax.ppermute(got_z, ("xlo", "xhi"), flip4)
    cells = swap(to_z, Z)
    cells = cells.reshape(128, D_T)
    pooled = (jnp.dot(counts, cells, preferred_element_type=F32) * 0.25).astype(BF16)

    pooled, got_x = lax.optimization_barrier((pooled, got_x))
    got = [got_x, got_z, got_xz]
    got += [lax.ppermute(piece, "core", flip2) for piece in got]
    scores_s, exp_s, total_s = student_score(student_rows, student_prompts, got)
    pooled = spread(pooled, ("y", "zh"), 16).reshape(ROWS, D_T)

    exp_t, exp_s, prompts, total = teacher_score(
        pooled, scores_s, exp_s, total_s, teacher_prompts, student_prompts, got
    )
    stats = spread(total, ("y", "zh"), 16)
    grad_term, place = gradient(exp_t, exp_s, total, stats, prompts)

    grad = exchange_sum(grad_term, "y", starts_y)
    others = [
        lax.ppermute(place, "zl", flip2),
        lax.ppermute(place, "xhi", flip2),
        lax.ppermute(place, ("xhi", "zl"), flip4),
    ]
    grad = exchange_sum(grad, "zh", starts_z).astype(BF16)
    patch_kl = ((place + others[0]) + others[1]) + others[2]
    grad, patch_kl = lax.optimization_barrier((grad, patch_kl))
    grad = spread(grad, Z, n_z)
    grad = spread(grad, ("xhi", "y"), n_w)
    patch_grad = grad.reshape(n_w, 4, 2, 16, D_S).transpose(1, 0, 2, 3, 4)

    return patch_kl, patch_grad.reshape(student_patches.shape)


def solution(mesh):
    split = Mesh(mesh.devices.reshape(2, 2, 2, 4, 4, 2), IMG + PRM)
    placed = (
        P(IMG, PRM, None),
        P(),
        P(IMG),
        P(PRM, None),
        P(IMG, None, None),
        P(PRM, None),
    )
    return jax.shard_map(
        body,
        mesh=split,
        in_specs=placed,
        out_specs=(P(IMG, None), P(IMG, None, None)),
        check_vma=False,
    )
```

```python
import functools

import jax
import jax.numpy as jnp
from jax import lax
from jax.experimental import pallas as pl
from jax.experimental.pallas import tpu as pltpu
from jax.sharding import Mesh, PartitionSpec as P

IMG = ("xlo", "core")
PRM = ("xhi", "y", "zh", "zl")
Z = ("zh", "zl")
F32 = jnp.float32
BF16 = jnp.bfloat16
D_T = 1152
D_S = 768
PIECE = 256
ROWS = 256
CONTRACT_LAST = (((1,), (1,)), ((), ()))
CONTRACT_FIRST = (((0,), (0,)), ((), ()))


def swap(x, axis):
    return lax.all_to_all(x, axis, split_axis=0, concat_axis=0, tiled=True)


def spread(x, axis, size):
    return swap(jnp.broadcast_to(x[None], (size,) + x.shape), axis)


def exchange_sum(x, axis, starts):
    rows = x.shape[0] // 4
    total = lax.dynamic_slice_in_dim(x, starts[0], rows, 0, allow_negative_indices=False)
    for k in range(1, 4):
        part = lax.dynamic_slice_in_dim(x, starts[k], rows, 0, allow_negative_indices=False)
        total = total + lax.ppermute(part, axis, [(i, i ^ k) for i in range(4)])
    return total


def half_kernel(teacher, student, half, sems):
    rows = pl.ds(lax.axis_index("core") * PIECE, PIECE)
    copies = [
        pltpu.make_async_copy(teacher.at[rows], half.at[:, 0:D_T], sems.at[0]),
        pltpu.make_async_copy(student.at[rows], half.at[:, D_T : D_T + D_S], sems.at[1]),
    ]
    for c in copies:
        c.start()
    for c in copies:
        c.wait()


def core_half(teacher, student):
    hbm = pl.BlockSpec(memory_space=pltpu.HBM)
    return pl.pallas_call(
        half_kernel,
        in_specs=[hbm, hbm],
        out_specs=pl.BlockSpec(memory_space=pltpu.VMEM),
        out_shape=pltpu.VMEM((PIECE, D_T + D_S), BF16),
        scratch_shapes=[pltpu.SemaphoreType.DMA((2,))],
        name="half",
    )(teacher, student)


def student_kernel(student_rows, own_s, *refs):
    got, (out, total, student, prompts, logits, sems) = refs[:6], refs[6:]
    copies = []

    def copy(source, target):
        copies.append(pltpu.make_async_copy(source, target, sems.at[len(copies)]))
        copies[-1].start()

    copy(student_rows, student)
    copy(own_s, prompts.at[0 : 2 * PIECE])
    for i, piece in enumerate(got):
        at = (2 + i) * PIECE
        copy(piece.at[:, D_T : D_T + D_S], prompts.at[at : at + PIECE])
    spans = [(0, 2 * PIECE, copies[:2]), (2 * PIECE, 8 * PIECE, copies[2:])]
    sent = len(copies)
    scores = []
    for first, last, needed in spans:
        for c in needed:
            c.wait()
        scores.append(
            lax.dot_general(
                prompts[first:last], student[...], CONTRACT_LAST, preferred_element_type=F32
            )
        )
        logits[first:last] = scores[-1]
        copy(logits.at[first:last], out.at[first:last])
    top = functools.reduce(jnp.maximum, [jnp.max(x, axis=0, keepdims=True) for x in scores])
    sums = sum(jnp.sum(jnp.exp(x - top), axis=0, keepdims=True) for x in scores)
    zero = jnp.zeros_like(top)
    for i, v in enumerate((top, sums) + (zero,) * 6):
        total[i : i + 1] = v
    for c in copies[sent:]:
        c.wait()


def student_score(student, own_s, got):
    hbm = pl.BlockSpec(memory_space=pltpu.HBM)
    in_hbm = [pltpu.with_memory_space_constraint(x, pltpu.HBM) for x in (student, own_s, *got)]
    return pl.pallas_call(
        student_kernel,
        in_specs=[hbm] * 8,
        out_specs=[hbm, pl.BlockSpec(memory_space=pltpu.VMEM)],
        out_shape=[
            pltpu.HBM((8 * PIECE, ROWS), F32),
            jax.ShapeDtypeStruct((8, ROWS), F32),
        ],
        scratch_shapes=[
            pltpu.VMEM((ROWS, D_S), BF16),
            pltpu.VMEM((8 * PIECE, D_S), BF16),
            pltpu.VMEM((8 * PIECE, ROWS), F32),
            pltpu.SemaphoreType.DMA((10,)),
        ],
        compiler_params=pltpu.CompilerParams(vmem_limit_bytes=24 << 20),
        cost_estimate=pl.CostEstimate(
            flops=2 * 8 * PIECE * ROWS * D_S, bytes_accessed=6 << 20, transcendentals=0
        ),
        name="student",
    )(*in_hbm)


def teacher_kernel(pooled, total_s, own_t, scores_s, own_s, *refs):
    got, (exp_t, exp_s, prompts, total, teacher, student, sems) = refs[:6], refs[6:]
    copies = []

    def copy(source, target):
        copies.append(pltpu.make_async_copy(source, target, sems.at[len(copies)]))
        copies[-1].start()

    copy(own_t, teacher.at[0 : 2 * PIECE])
    for i, piece in enumerate(got):
        at = (2 + i) * PIECE
        copy(piece.at[:, 0:D_T], teacher.at[at : at + PIECE])
    copy(scores_s, student)
    copy(own_s, prompts.at[0 : 2 * PIECE])
    for i, piece in enumerate(got):
        at = (2 + i) * PIECE
        copy(piece.at[:, D_T : D_T + D_S], prompts.at[at : at + PIECE])

    spans = [(0, 2 * PIECE, copies[:1]), (2 * PIECE, 8 * PIECE, copies[1:7])]
    logits = []
    for first, last, needed in spans:
        for c in needed:
            c.wait()
        logits.append(
            lax.dot_general(
                teacher[first:last], pooled[...], CONTRACT_LAST, preferred_element_type=F32
            )
        )
    max_t = functools.reduce(jnp.maximum, [jnp.max(x, axis=0, keepdims=True) for x in logits])
    copies[7].wait()
    max_s, sum_s = total_s[0:1], total_s[1:2]
    sum_t = number = 0.0
    for (first, last, _), scores in zip(spans, logits):
        e_t = jnp.exp(scores - max_t)
        exp_t[first:last] = e_t
        sum_t += jnp.sum(e_t, axis=0, keepdims=True)
        number += jnp.sum(e_t * (scores - student[first:last]), axis=0, keepdims=True)
        exp_s[first:last] = jnp.exp(student[first:last] - max_s)
    zero = jnp.zeros_like(max_t)
    for i, v in enumerate((max_t, max_t, max_s, zero, sum_t, number, sum_s, zero)):
        total[i : i + 1] = v
    for c in copies[8:]:
        c.wait()


def teacher_score(pooled, scores_s, total_s, own_t, own_s, got):
    vmem = pl.BlockSpec(memory_space=pltpu.VMEM)
    hbm = pl.BlockSpec(memory_space=pltpu.HBM)
    in_hbm = [
        pltpu.with_memory_space_constraint(x, pltpu.HBM)
        for x in (own_t, scores_s, own_s, *got)
    ]
    return pl.pallas_call(
        teacher_kernel,
        in_specs=[vmem, vmem] + [hbm] * 9,
        out_specs=[vmem] * 4,
        out_shape=[
            jax.ShapeDtypeStruct((8 * PIECE, ROWS), F32),
            jax.ShapeDtypeStruct((8 * PIECE, ROWS), F32),
            jax.ShapeDtypeStruct((8 * PIECE, D_S), BF16),
            jax.ShapeDtypeStruct((8, ROWS), F32),
        ],
        scratch_shapes=[
            pltpu.VMEM((8 * PIECE, D_T), BF16),
            pltpu.VMEM((8 * PIECE, ROWS), F32),
            pltpu.SemaphoreType.DMA((15,)),
        ],
        compiler_params=pltpu.CompilerParams(vmem_limit_bytes=24 << 20),
        cost_estimate=pl.CostEstimate(
            flops=2 * 8 * PIECE * ROWS * D_T, bytes_accessed=14 << 20, transcendentals=0
        ),
        name="teacher",
    )(pooled, total_s, *in_hbm)


def grad_kernel(exp_t, exp_s, mine, stats, prompts, grad, kl):
    every = stats[...]
    top = jnp.max(every, axis=0)
    weight = pltpu.roll(jnp.exp(every - top[None]), 4, 1)
    total = jnp.sum(every * weight, axis=0)
    top_t, top_s = top[0:1], top[2:3]
    sum_t, number, sum_s = total[4:5], total[5:6], total[6:7]
    rows = number / sum_t - top_t - jnp.log(sum_t) + top_s + jnp.log(sum_s)
    rows = jnp.broadcast_to(rows, (8, ROWS))
    image = lax.broadcasted_iota(jnp.int32, rows.shape, 0)
    lane = lax.broadcasted_iota(jnp.int32, rows.shape, 1)
    placed = jnp.zeros_like(rows)
    for i in range(4):
        for y in range(4):
            moved = pltpu.roll(rows, (32 * y - 64 * y - 16 * i) % ROWS, 1)
            here = (image == i) & (lane >= 32 * y) & (lane < 32 * y + 16)
            placed = jnp.where(here, moved, placed)
    first = lax.axis_index("xhi") * 128 + lax.axis_index("zl") * 16
    kl[...] = pltpu.roll(placed, first, 1)[0:4]
    scale_t = jnp.exp(mine[0:1] - top_t) / sum_t
    scale_s = jnp.exp(mine[2:3] - top_s) / sum_s
    difference = (exp_s[...] * scale_s - exp_t[...] * scale_t).astype(BF16)
    grad[...] = lax.dot_general(
        difference, prompts[...], CONTRACT_FIRST, preferred_element_type=F32
    )


def gradient(exp_t, exp_s, mine, stats, prompts):
    vmem = pl.BlockSpec(memory_space=pltpu.VMEM)
    return pl.pallas_call(
        grad_kernel,
        in_specs=[vmem] * 5,
        out_specs=[vmem] * 2,
        out_shape=[
            jax.ShapeDtypeStruct((ROWS, D_S), F32),
            jax.ShapeDtypeStruct((4, ROWS), F32),
        ],
        compiler_params=pltpu.CompilerParams(vmem_limit_bytes=24 << 20),
        cost_estimate=pl.CostEstimate(
            flops=2 * 8 * PIECE * ROWS * D_S, bytes_accessed=8 << 20, transcendentals=0
        ),
        name="gradient",
    )(exp_t, exp_s, mine, stats, prompts)


def body(teacher_maps, pool_index, pairing, teacher_prompts, student_patches, student_prompts):
    n_w, n_z = 8, 8
    xhi, y, zh, zl = (lax.axis_index(a) for a in PRM)
    w = xhi * 4 + y
    z = zh * 2 + zl

    half = core_half(teacher_prompts, student_prompts)
    flip2, flip4 = ([(i, n - 1 - i) for i in range(n)] for n in (2, 4))
    teacher_maps, half = lax.optimization_barrier((teacher_maps, half))
    got_z = lax.ppermute(half, "zl", flip2)
    got_x = lax.ppermute(half, ("xlo", "xhi"), flip4)

    patches = student_patches.reshape(4, 2, 4, 2, 16, D_S)
    patches = lax.dynamic_index_in_dim(patches, xhi, 1, keepdims=False)
    patches = lax.dynamic_index_in_dim(patches, zl, 2, keepdims=False)
    student_rows = patches.transpose(1, 0, 2, 3).reshape(ROWS, D_S)

    source = jnp.arange(8)
    grid_row = 4 * w + source // 2
    grid_row = jnp.where(
        zl == 0,
        jnp.where(source >= 6, 4 * w - 1, grid_row),
        jnp.where(source <= 1, 4 * w + 4, grid_row),
    )
    cell_id = grid_row[:, None] * 32 + (source % 2)[:, None] * 16 + jnp.arange(16)[None]
    cell_id = cell_id.reshape(-1)
    index = lax.dynamic_slice_in_dim(pool_index, 16 * (2 * w + zl), 16, 0)
    counts = jnp.sum((index[:, :, None] == cell_id[None, None, :]).astype(F32), axis=1).astype(BF16)
    starts_y = [(y ^ k) * 64 for k in range(4)]
    starts_z = [(zh ^ k) * 16 for k in range(4)]

    every_map = lax.all_gather(teacher_maps, IMG, axis=0, tiled=True)
    wanted = pairing[:, None] == jnp.arange(16)[None]
    owned = jnp.sum(jnp.where(wanted[:, :, None, None], every_map[None], 0), axis=1, dtype=BF16)
    pairs = [((v + 1) * n_z + c, v * n_z + c) for v in range(n_w - 1) for c in (0, 1)]
    pairs += [(v * n_z + c, (v + 1) * n_z + c) for v in range(n_w - 1) for c in (6, 7)]
    halo = lax.ppermute(owned, PRM, pairs)
    lower = jnp.arange(2)[None, :, None, None] == 1
    outside = jnp.where(lower, z <= 1, z >= 6)
    to_z = jnp.where(outside, halo[:, None], owned[:, None]).reshape((8,) + owned.shape[1:])
    to_z, got_z, counts, starts_y, starts_z = lax.optimization_barrier(
        (to_z, got_z, counts, starts_y, starts_z)
    )
    got_xz = lax.ppermute(got_z, ("xlo", "xhi"), flip4)
    cells = swap(to_z, Z)
    cells = cells.reshape(128, D_T)
    pooled = (jnp.dot(counts, cells, preferred_element_type=F32) * 0.25).astype(BF16)

    pooled, got_x = lax.optimization_barrier((pooled, got_x))
    got = [got_x, got_z, got_xz]
    got += [lax.ppermute(piece, "core", flip2) for piece in got]
    scores_s, total_s = student_score(student_rows, student_prompts, got)
    pooled = spread(pooled, ("y", "zh"), 16).reshape(ROWS, D_T)

    exp_t, exp_s, prompts, total = teacher_score(
        pooled, scores_s, total_s, teacher_prompts, student_prompts, got
    )
    stats = spread(total, ("y", "zh"), 16)
    grad_term, place = gradient(exp_t, exp_s, total, stats, prompts)

    grad = exchange_sum(grad_term, "y", starts_y)
    others = [
        lax.ppermute(place, "zl", flip2),
        lax.ppermute(place, "xhi", flip2),
        lax.ppermute(place, ("xhi", "zl"), flip4),
    ]
    grad = exchange_sum(grad, "zh", starts_z).astype(BF16)
    patch_kl = ((place + others[0]) + others[1]) + others[2]
    grad, patch_kl = lax.optimization_barrier((grad, patch_kl))
    grad = spread(grad, "zh", 4)
    grad = spread(grad, ("xhi", "y", "zl"), 2 * n_w)
    patch_grad = grad.reshape(n_w, 2, 4, 16, D_S).transpose(2, 0, 1, 3, 4)

    return patch_kl, patch_grad.reshape(student_patches.shape)


def solution(mesh):
    split = Mesh(mesh.devices.reshape(2, 2, 2, 4, 4, 2), IMG + PRM)
    placed = (
        P(IMG, PRM, None),
        P(),
        P(IMG),
        P(PRM, None),
        P(IMG, None, None),
        P(PRM, None),
    )
    return jax.shard_map(
        body,
        mesh=split,
        in_specs=placed,
        out_specs=(P(IMG, None), P(IMG, None, None)),
        check_vma=False,
    )
```

```python
import functools

import jax
import jax.numpy as jnp
from jax import lax
from jax.experimental import pallas as pl
from jax.experimental.pallas import tpu as pltpu
from jax.sharding import Mesh, PartitionSpec as P

IMG = ("xlo", "core")
PRM = ("xhi", "y", "zh", "zl")
Z = ("zh", "zl")
F32 = jnp.float32
BF16 = jnp.bfloat16
D_T = 1152
D_S = 768
PIECE = 256
ROWS = 256
CONTRACT_LAST = (((1,), (1,)), ((), ()))
CONTRACT_FIRST = (((0,), (0,)), ((), ()))


def swap(x, axis):
    return lax.all_to_all(x, axis, split_axis=0, concat_axis=0, tiled=True)


def spread(x, axis, size):
    return swap(jnp.broadcast_to(x[None], (size,) + x.shape), axis)


def exchange_sum(x, axis, starts):
    rows = x.shape[0] // 4
    total = lax.dynamic_slice_in_dim(x, starts[0], rows, 0, allow_negative_indices=False)
    for k in (2, 1, 3):
        part = lax.dynamic_slice_in_dim(x, starts[k], rows, 0, allow_negative_indices=False)
        total = total + lax.ppermute(part, axis, [(i, i ^ k) for i in range(4)])
    return total


def half_kernel(teacher, student, half, sems):
    rows = pl.ds(lax.axis_index("core") * PIECE, PIECE)
    copies = [
        pltpu.make_async_copy(teacher.at[rows], half.at[:, 0:D_T], sems.at[0]),
        pltpu.make_async_copy(student.at[rows], half.at[:, D_T : D_T + D_S], sems.at[1]),
    ]
    for c in copies:
        c.start()
    for c in copies:
        c.wait()


def core_half(teacher, student):
    hbm = pl.BlockSpec(memory_space=pltpu.HBM)
    return pl.pallas_call(
        half_kernel,
        in_specs=[hbm, hbm],
        out_specs=pl.BlockSpec(memory_space=pltpu.VMEM),
        out_shape=pltpu.VMEM((PIECE, D_T + D_S), BF16),
        scratch_shapes=[pltpu.SemaphoreType.DMA((2,))],
        name="half",
    )(teacher, student)


def student_kernel(student_rows, own_s, *refs):
    got, (out, total, student, prompts, logits, sems) = refs[:6], refs[6:]
    copies = []

    def copy(source, target):
        copies.append(pltpu.make_async_copy(source, target, sems.at[len(copies)]))
        copies[-1].start()

    copy(student_rows, student)
    copy(own_s, prompts.at[0 : 2 * PIECE])
    for i, piece in enumerate(got):
        at = (2 + i) * PIECE
        copy(piece.at[:, D_T : D_T + D_S], prompts.at[at : at + PIECE])
    spans = [(0, 2 * PIECE, copies[:2]), (2 * PIECE, 8 * PIECE, copies[2:])]
    sent = len(copies)
    scores = []
    for first, last, needed in spans:
        for c in needed:
            c.wait()
        scores.append(
            lax.dot_general(
                prompts[first:last], student[...], CONTRACT_LAST, preferred_element_type=F32
            )
        )
        logits[first:last] = scores[-1]
        copy(logits.at[first:last], out.at[first:last])
    top = functools.reduce(jnp.maximum, [jnp.max(x, axis=0, keepdims=True) for x in scores])
    sums = sum(jnp.sum(jnp.exp(x - top), axis=0, keepdims=True) for x in scores)
    zero = jnp.zeros_like(top)
    for i, v in enumerate((top, sums) + (zero,) * 6):
        total[i : i + 1] = v
    for c in copies[sent:]:
        c.wait()


def student_score(student, own_s, got):
    hbm = pl.BlockSpec(memory_space=pltpu.HBM)
    in_hbm = [pltpu.with_memory_space_constraint(x, pltpu.HBM) for x in (student, own_s, *got)]
    return pl.pallas_call(
        student_kernel,
        in_specs=[hbm] * 8,
        out_specs=[hbm, pl.BlockSpec(memory_space=pltpu.VMEM)],
        out_shape=[
            pltpu.HBM((8 * PIECE, ROWS), F32),
            jax.ShapeDtypeStruct((8, ROWS), F32),
        ],
        scratch_shapes=[
            pltpu.VMEM((ROWS, D_S), BF16),
            pltpu.VMEM((8 * PIECE, D_S), BF16),
            pltpu.VMEM((8 * PIECE, ROWS), F32),
            pltpu.SemaphoreType.DMA((10,)),
        ],
        compiler_params=pltpu.CompilerParams(vmem_limit_bytes=24 << 20),
        cost_estimate=pl.CostEstimate(
            flops=2 * 8 * PIECE * ROWS * D_S, bytes_accessed=6 << 20, transcendentals=0
        ),
        name="student",
    )(*in_hbm)


def teacher_kernel(pooled, total_s, own_t, scores_s, own_s, *refs):
    got, (exp_t, exp_s, prompts, total, teacher, student, sems) = refs[:6], refs[6:]
    copies = []

    def copy(source, target):
        copies.append(pltpu.make_async_copy(source, target, sems.at[len(copies)]))
        copies[-1].start()

    copy(own_t, teacher.at[0 : 2 * PIECE])
    for i, piece in enumerate(got):
        at = (2 + i) * PIECE
        copy(piece.at[:, 0:D_T], teacher.at[at : at + PIECE])
    copy(scores_s, student)
    copy(own_s, prompts.at[0 : 2 * PIECE])
    for i, piece in enumerate(got):
        at = (2 + i) * PIECE
        copy(piece.at[:, D_T : D_T + D_S], prompts.at[at : at + PIECE])

    spans = [(0, 2 * PIECE, copies[:1]), (2 * PIECE, 8 * PIECE, copies[1:7])]
    logits = []
    for first, last, needed in spans:
        for c in needed:
            c.wait()
        logits.append(
            lax.dot_general(
                teacher[first:last], pooled[...], CONTRACT_LAST, preferred_element_type=F32
            )
        )
    max_t = functools.reduce(jnp.maximum, [jnp.max(x, axis=0, keepdims=True) for x in logits])
    copies[7].wait()
    max_s, sum_s = total_s[0:1], total_s[1:2]
    sum_t = number = 0.0
    for (first, last, _), scores in zip(spans, logits):
        e_t = jnp.exp(scores - max_t)
        exp_t[first:last] = e_t
        sum_t += jnp.sum(e_t, axis=0, keepdims=True)
        number += jnp.sum(e_t * (scores - student[first:last]), axis=0, keepdims=True)
        exp_s[first:last] = jnp.exp(student[first:last] - max_s)
    zero = jnp.zeros_like(max_t)
    for i, v in enumerate((max_t, max_t, max_s, zero, sum_t, number, sum_s, zero)):
        total[i : i + 1] = v
    for c in copies[8:]:
        c.wait()


def teacher_score(pooled, scores_s, total_s, own_t, own_s, got):
    vmem = pl.BlockSpec(memory_space=pltpu.VMEM)
    hbm = pl.BlockSpec(memory_space=pltpu.HBM)
    in_hbm = [
        pltpu.with_memory_space_constraint(x, pltpu.HBM)
        for x in (own_t, scores_s, own_s, *got)
    ]
    return pl.pallas_call(
        teacher_kernel,
        in_specs=[vmem, vmem] + [hbm] * 9,
        out_specs=[vmem] * 4,
        out_shape=[
            jax.ShapeDtypeStruct((8 * PIECE, ROWS), F32),
            jax.ShapeDtypeStruct((8 * PIECE, ROWS), F32),
            jax.ShapeDtypeStruct((8 * PIECE, D_S), BF16),
            jax.ShapeDtypeStruct((8, ROWS), F32),
        ],
        scratch_shapes=[
            pltpu.VMEM((8 * PIECE, D_T), BF16),
            pltpu.VMEM((8 * PIECE, ROWS), F32),
            pltpu.SemaphoreType.DMA((15,)),
        ],
        compiler_params=pltpu.CompilerParams(vmem_limit_bytes=24 << 20),
        cost_estimate=pl.CostEstimate(
            flops=2 * 8 * PIECE * ROWS * D_T, bytes_accessed=14 << 20, transcendentals=0
        ),
        name="teacher",
    )(pooled, total_s, *in_hbm)


def grad_kernel(exp_t, exp_s, mine, stats, prompts, grad, kl):
    every = stats[...]
    top = jnp.max(every, axis=0)
    weight = pltpu.roll(jnp.exp(every - top[None]), 4, 1)
    total = jnp.sum(every * weight, axis=0)
    top_t, top_s = top[0:1], top[2:3]
    sum_t, number, sum_s = total[4:5], total[5:6], total[6:7]
    rows = number / sum_t - top_t - jnp.log(sum_t) + top_s + jnp.log(sum_s)
    rows = jnp.broadcast_to(rows, (8, ROWS))
    image = lax.broadcasted_iota(jnp.int32, rows.shape, 0)
    lane = lax.broadcasted_iota(jnp.int32, rows.shape, 1)
    placed = jnp.zeros_like(rows)
    for i in range(4):
        for y in range(4):
            moved = pltpu.roll(rows, (32 * y - 64 * y - 16 * i) % ROWS, 1)
            here = (image == i) & (lane >= 32 * y) & (lane < 32 * y + 16)
            placed = jnp.where(here, moved, placed)
    first = lax.axis_index("xhi") * 128 + lax.axis_index("zl") * 16
    kl[...] = pltpu.roll(placed, first, 1)[0:4]
    scale_t = jnp.exp(mine[0:1] - top_t) / sum_t
    scale_s = jnp.exp(mine[2:3] - top_s) / sum_s
    difference = (exp_s[...] * scale_s - exp_t[...] * scale_t).astype(BF16)
    grad[...] = lax.dot_general(
        difference, prompts[...], CONTRACT_FIRST, preferred_element_type=F32
    )


def gradient(exp_t, exp_s, mine, stats, prompts):
    vmem = pl.BlockSpec(memory_space=pltpu.VMEM)
    return pl.pallas_call(
        grad_kernel,
        in_specs=[vmem] * 5,
        out_specs=[vmem] * 2,
        out_shape=[
            jax.ShapeDtypeStruct((ROWS, D_S), F32),
            jax.ShapeDtypeStruct((4, ROWS), F32),
        ],
        compiler_params=pltpu.CompilerParams(vmem_limit_bytes=24 << 20),
        cost_estimate=pl.CostEstimate(
            flops=2 * 8 * PIECE * ROWS * D_S, bytes_accessed=8 << 20, transcendentals=0
        ),
        name="gradient",
    )(exp_t, exp_s, mine, stats, prompts)


def body(teacher_maps, pool_index, pairing, teacher_prompts, student_patches, student_prompts):
    n_w, n_z = 8, 8
    xhi, y, zh, zl = (lax.axis_index(a) for a in PRM)
    w = xhi * 4 + y
    z = zh * 2 + zl

    half = core_half(teacher_prompts, student_prompts)
    flip2, flip4 = ([(i, n - 1 - i) for i in range(n)] for n in (2, 4))
    teacher_maps, half = lax.optimization_barrier((teacher_maps, half))
    got_z = lax.ppermute(half, "zl", flip2)
    got_x = lax.ppermute(half, ("xlo", "xhi"), flip4)

    patches = student_patches.reshape(4, 2, 4, 2, 16, D_S)
    patches = lax.dynamic_index_in_dim(patches, xhi, 1, keepdims=False)
    patches = lax.dynamic_index_in_dim(patches, zl, 2, keepdims=False)
    student_rows = patches.transpose(1, 0, 2, 3).reshape(ROWS, D_S)

    source = jnp.arange(8)
    grid_row = 4 * w + source // 2
    grid_row = jnp.where(
        zl == 0,
        jnp.where(source >= 6, 4 * w - 1, grid_row),
        jnp.where(source <= 1, 4 * w + 4, grid_row),
    )
    cell_id = grid_row[:, None] * 32 + (source % 2)[:, None] * 16 + jnp.arange(16)[None]
    cell_id = cell_id.reshape(-1)
    index = lax.dynamic_slice_in_dim(pool_index, 16 * (2 * w + zl), 16, 0)
    counts = jnp.sum((index[:, :, None] == cell_id[None, None, :]).astype(F32), axis=1).astype(BF16)
    starts_y = [(y ^ k) * 64 for k in range(4)]
    starts_z = [(zh ^ k) * 16 for k in range(4)]

    every_map = lax.all_gather(teacher_maps, IMG, axis=0, tiled=True)
    wanted = pairing[:, None] == jnp.arange(16)[None]
    owned = jnp.sum(jnp.where(wanted[:, :, None, None], every_map[None], 0), axis=1, dtype=BF16)
    pairs = [((v + 1) * n_z + c, v * n_z + c) for v in range(n_w - 1) for c in (0, 1)]
    pairs += [(v * n_z + c, (v + 1) * n_z + c) for v in range(n_w - 1) for c in (6, 7)]
    halo = lax.ppermute(owned, PRM, pairs)
    lower = jnp.arange(2)[None, :, None, None] == 1
    outside = jnp.where(lower, z <= 1, z >= 6)
    to_z = jnp.where(outside, halo[:, None], owned[:, None]).reshape((8,) + owned.shape[1:])
    to_z, got_z, counts, starts_y, starts_z = lax.optimization_barrier(
        (to_z, got_z, counts, starts_y, starts_z)
    )
    got_xz = lax.ppermute(got_z, ("xlo", "xhi"), flip4)
    cells = swap(to_z, Z)
    cells = cells.reshape(128, D_T)
    pooled = (jnp.dot(counts, cells, preferred_element_type=F32) * 0.25).astype(BF16)

    pooled, got_x = lax.optimization_barrier((pooled, got_x))
    got = [got_x, got_z, got_xz]
    got += [lax.ppermute(piece, "core", flip2) for piece in got]
    scores_s, total_s = student_score(student_rows, student_prompts, got)
    pooled = spread(pooled, ("y", "zh"), 16).reshape(ROWS, D_T)

    exp_t, exp_s, prompts, total = teacher_score(
        pooled, scores_s, total_s, teacher_prompts, student_prompts, got
    )
    stats = spread(total, ("y", "zh"), 16)
    grad_term, place = gradient(exp_t, exp_s, total, stats, prompts)

    grad = exchange_sum(grad_term, "y", starts_y)
    others = [
        lax.ppermute(place, "zl", flip2),
        lax.ppermute(place, "xhi", flip2),
        lax.ppermute(place, ("xhi", "zl"), flip4),
    ]
    grad = exchange_sum(grad, "zh", starts_z).astype(BF16)
    patch_kl = ((place + others[0]) + others[1]) + others[2]
    grad, patch_kl = lax.optimization_barrier((grad, patch_kl))
    grad = spread(grad, "zh", 4)
    grad = spread(grad, ("xhi", "y", "zl"), 2 * n_w)
    patch_grad = grad.reshape(n_w, 2, 4, 16, D_S).transpose(2, 0, 1, 3, 4)

    return patch_kl, patch_grad.reshape(student_patches.shape)


def solution(mesh):
    split = Mesh(mesh.devices.reshape(2, 2, 2, 4, 4, 2), IMG + PRM)
    placed = (
        P(IMG, PRM, None),
        P(),
        P(IMG),
        P(PRM, None),
        P(IMG, None, None),
        P(PRM, None),
    )
    return jax.shard_map(
        body,
        mesh=split,
        in_specs=placed,
        out_specs=(P(IMG, None), P(IMG, None, None)),
        check_vma=False,
    )
```
